128 devices in a mesh: aux: 16 (over y, x), orb: 8 (over z, core).
Axes of the slice: x: 4, y: 4, z: 4, core: 2. Of those that a mesh axis runs over, the one named last changes fastest.
Arguments:
- three_center: bfloat16 [64, 8, 64, 32, 128], P('aux'), may hold values from -0.5 to 0.5
- orbitals: bfloat16 [32768, 1024], P('aux', 'orb'), may hold values from -6 to 6
- partners: int32 [64, 8, 4], P('aux'), may hold values from 0 to 1023, as said below
- pair_owner: int32 [64, 56], P('aux'), may hold values from 0 to 2047, as said below
Outputs:
- exchange: float32 [2048, 1024], P(('aux', 'orb'))
The draws below stay inside these ranges and needn't reach their ends.
Inputs may be any that keep to these rules, and one draw needn't show every extreme that they name: `partners`: basis block b is held by index b // 64 of aux. Of the 128 partner entries of the auxiliary blocks of one index of aux, at most 16 name blocks held by one index of aux; in every draw each index of aux has exactly 16 entries naming blocks of one index of aux. `pair_owner`: exchange block q belongs to owner device q // 16 (owners numbered aux index times the size of orb plus orb index). Of the 224 entries of the auxiliary blocks of one index of aux, at most 3 name blocks of one owner device; in every draw one owner device receives exactly 3 entries from every index of aux.
All inputs are finite; a program needn't handle non-finite values.
Results may differ from the reference program's by a relative error of at most 0.004.
Values may be sent and summed in bfloat16 or wider, within the bound.
No kernel may reach another device: no remote copies, remote signals or barrier semaphores. Data moves between devices by JAX's collectives and lax.ppermute only.
A program may use at most 128 MiB of HBM per device.

```python
import jax
import jax.numpy as jnp
import numpy as np
from jax import lax

BS = 32
PA = 64
MS = 8
NPS = 4
AUX_DEV = 4
NOCC = 1024
BLK_DEV = 64
OWN_DEV = 16
NBLK = 1024
NBAS = 32768
NAUXB = 64
EP = 56
E = 224
CAP = 3
FETCH = 16
NPAIR = 2048


def draw_partners(key, part):
    key = jax.random.fold_in(key, 23)
    source_count = NBLK // BLK_DEV
    group_count = NAUXB // AUX_DEV
    entries = AUX_DEV * MS * NPS

    def one_group(group_key):
        key_full, key_pool, key_order, key_local = jax.random.split(group_key, 4)
        full_source = jax.random.randint(key_full, (), 0, source_count).astype(jnp.int32)
        others = (full_source + 1 + jnp.arange(source_count - 1, dtype=jnp.int32)) % source_count
        pool = jax.random.permutation(key_pool, jnp.tile(others, FETCH))[:entries - FETCH]
        sources = jnp.concatenate([jnp.full((FETCH,), 0, jnp.int32) + full_source, pool])
        sources = jax.random.permutation(key_order, sources)
        local = jax.random.randint(key_local, (entries,), 0, BLK_DEV).astype(jnp.int32)
        return sources * BLK_DEV + local
    rows = jax.vmap(one_group)(jax.random.split(key, group_count))
    return rows.reshape(NAUXB, MS, NPS).astype(jnp.int32)


def draw_pair_owner(key, part):
    key = jax.random.fold_in(key, 11)
    owner_count = NPAIR // OWN_DEV
    group_count = NAUXB // AUX_DEV
    key_full, key_groups = jax.random.split(key, 2)
    full_owner = jax.random.randint(key_full, (), 0, owner_count).astype(jnp.int32)

    def one_group(group_key):
        key_pool, key_order, key_local = jax.random.split(group_key, 3)
        others = (full_owner + 1 + jnp.arange(owner_count - 1, dtype=jnp.int32)) % owner_count
        pool = jax.random.permutation(key_pool, jnp.tile(others, CAP))[:E - CAP]
        owners = jnp.concatenate([jnp.full((CAP,), 0, jnp.int32) + full_owner, pool])
        owners = jax.random.permutation(key_order, owners)
        local = jax.random.randint(key_local, (E,), 0, OWN_DEV).astype(jnp.int32)
        return owners * OWN_DEV + local
    rows = jax.vmap(one_group)(jax.random.split(key_groups, group_count))
    return rows.reshape(NAUXB, EP).astype(jnp.int32)


def shard_levels(rng, dims, pieces, least, high):
    def one(axis_at, shards_of):
        heights = jax.random.uniform(jax.random.fold_in(jax.random.fold_in(rng, 6), axis_at), (shards_of,), jnp.float32, least / len(pieces), high / len(pieces))
        return jnp.repeat(jnp.exp(heights), dims[axis_at] // shards_of).reshape((-1,) + (1,) * (len(dims) - axis_at - 1))

    factor_of = one(*pieces[0])
    for cut in pieces[1:]:
        factor_of = factor_of * one(*cut)
    return factor_of


def bell_draw(stream_key, extent, scale, limit, pieces=(), kind=jnp.bfloat16):
    gain = shard_levels(stream_key, extent, pieces, -0.22, 0.18) if pieces else 1.0
    values = jax.random.normal(stream_key, extent, jnp.float32) * scale * gain
    return jnp.minimum(jnp.maximum(values, -limit), limit).astype(kind)


def setup_inputs(seed: int = 0) -> dict:
    arg_keys = jax.random.split(jax.random.key(seed), 5)
    return {
        "three_center": bell_draw(arg_keys[0], (NAUXB, MS, PA, BS, NPS * BS), (NPS * BS) ** -0.5, 0.5, ((0, 16),)),
        "orbitals": bell_draw(arg_keys[1], (NBAS, NOCC), 1.0, 6.0, ((0, 16), (1, 8))),
        "partners": draw_partners(jax.random.fold_in(arg_keys[4], 71), 0),
        "pair_owner": draw_pair_owner(jax.random.fold_in(arg_keys[4], 71), 0),
    }


def cross_slots(count):
    return np.array([first * count + second for first in range(count) for second in range(count) if first != second], dtype=np.int32)

def reference(three_center, orbitals, partners, pair_owner):
    coeff_blocks = orbitals.reshape(NBLK, BS, NOCC)
    offdiag_index = cross_slots(MS)
    factor = 1.0 / np.sqrt(PA * NOCC)

    def one_block(operands):
        tensor, partner_ids = operands
        picked = coeff_blocks[partner_ids].reshape(MS, NPS * BS, NOCC)
        half = jnp.einsum('saml,slo->samo', tensor.astype(jnp.float32), picked.astype(jnp.float32), precision=lax.Precision.HIGHEST)
        half = half.astype(jnp.bfloat16).astype(jnp.float32)
        blocks = jnp.einsum('samo,tano->stmn', half, half, precision=lax.Precision.HIGHEST)
        blocks = blocks.reshape(MS * MS, BS * BS)
        return blocks[offdiag_index] * factor
    partial_value = lax.map(one_block, (three_center, partners))
    return jax.ops.segment_sum(partial_value.reshape(-1, BS * BS), pair_owner.reshape(-1), num_segments=NPAIR)
```

```python
import functools

import jax
import jax.numpy as jnp
import numpy as np
from jax import lax
from jax.experimental import pallas as pl
from jax.experimental.pallas import tpu as pltpu
from jax.sharding import PartitionSpec as P

BS = 32
PA = 64
MS = 8
NPS = 4
AUX_DEV = 4
NOCC = 1024
BLK_DEV = 64
OWN_DEV = 16
CAP = 3
FETCH = 16
EP = MS * (MS - 1)
E = AUX_DEV * EP
ENTRIES = AUX_DEV * MS * NPS
OCC = 128
SIDE = 4
AUX = SIDE * SIDE
ORB = 8
DEVS = AUX * ORB
ROW_CAP = SIDE * FETCH
ROWS = 8
CHUNK = 16
LANES = 128
AXES = ("aux", "orb")


def shifted(step, near):
    pairs = []
    for aux in range(AUX):
        x, y = aux % SIDE, aux // SIDE
        for orb in range(ORB):
            if (orb % 2 == 0) == near:
                to = y * SIDE + (x + step) % SIDE
            else:
                to = ((y + step) % SIDE) * SIDE + x
            pairs.append((aux * ORB + orb, to * ORB + orb))
    return pairs


def pack_kernel(req1, req2, req3, own, got1, got2, got3, out1, out2, out3, shards, sems):
    copies = [
        pltpu.make_async_copy(
            src, shards.at[pl.ds(at * BLK_DEV, BLK_DEV)], sems.at[at]
        )
        for at, src in enumerate((own, got1, got2, got3))
    ]
    for copy in copies:
        copy.start()
    for copy in copies:
        copy.wait()
    for req, out in ((req1, out1), (req2, out2), (req3, out3)):

        @pl.loop(0, ROW_CAP, unroll=8)
        def _(r):
            out[r] = shards[req[0, r]]


def pack(reqs, own, got):
    block = jax.ShapeDtypeStruct((ROW_CAP, BS, OCC), jnp.bfloat16)
    return pl.pallas_call(
        pack_kernel,
        out_shape=[block] * 3,
        in_specs=[pl.BlockSpec(memory_space=pltpu.SMEM)] * 3 + [pl.BlockSpec(memory_space=pl.ANY)] * 4,
        out_specs=[pl.BlockSpec(memory_space=pltpu.VMEM)] * 3,
        scratch_shapes=[
            pltpu.VMEM((SIDE * BLK_DEV, BS, OCC), jnp.bfloat16),
            pltpu.SemaphoreType.DMA((4,)),
        ],
        compiler_params=pltpu.CompilerParams(vmem_limit_bytes=32 * 1024 * 1024),
        cost_estimate=pl.CostEstimate(flops=0, bytes_accessed=4 * 1024 * 1024, transcendentals=0),
        name="pack",
    )(*reqs, own, *got)


def main_kernel(
    picks, slots, own, got1, got2, got3, row1, row2, row3, tensor, out,
    blocks, pairs, half, total, staged, sems,
):
    p, c = pl.program_id(0), pl.program_id(1)
    sources = (own, got1, got2, got3, row1, row2, row3)

    @pl.when((p == 0) & (c == 0))
    def _():
        copies = [
            pltpu.make_async_copy(src, blocks.at[pl.ds(at * BLK_DEV, BLK_DEV)], sems.at[at])
            for at, src in enumerate(sources)
        ]
        for copy in copies:
            copy.start()
        staged[...] = jnp.zeros_like(staged)
        pairs[...] = jnp.zeros_like(pairs)
        for copy in copies:
            copy.wait()

    @pl.when(c == 0)
    def _():
        total[...] = jnp.zeros_like(total)
        for s in range(MS):
            side = (s % 2) * OCC
            for k in range(NPS):
                pairs[s // 2, pl.ds(side + k * BS, BS), pl.ds(side, OCC)] = blocks[
                    picks[(p * MS + s) * NPS + k]
                ]

    for pair in range(MS // 2):
        left = jnp.concatenate(
            [tensor[0, 2 * pair + side].reshape(CHUNK * BS, OCC) for side in range(2)], axis=1
        )
        both = jnp.dot(left, pairs[pair], preferred_element_type=jnp.float32).astype(jnp.bfloat16)
        for side in range(2):
            for a in range(CHUNK):
                half[pl.ds((2 * pair + side) * BS, BS), pl.ds(a * OCC, OCC)] = both[
                    a * BS : (a + 1) * BS, side * OCC : (side + 1) * OCC
                ]
    everything = half[...]
    total[...] += lax.dot_general(
        everything, everything, (((1,), (1,)), ((), ())), preferred_element_type=jnp.float32
    )

    @pl.when(c == PA // CHUNK - 1)
    def _():
        factor = np.float32(1.0 / np.sqrt(PA * NOCC))
        e = 0
        for s in range(MS):
            for t in range(MS):
                if s == t:
                    continue
                tile = jnp.concatenate(
                    [
                        total[pl.ds(s * BS + j * ROWS, ROWS), pl.ds(t * BS, BS)]
                        for j in range(BS // ROWS)
                    ],
                    axis=1,
                )
                staged[slots[p * EP + e]] = tile * factor
                e += 1

    @pl.when((p == AUX_DEV - 1) & (c == PA // CHUNK - 1))
    def _():
        out[...] = staged[...].reshape(DEVS * CAP * ROWS, LANES).astype(jnp.bfloat16)


def products(picks, slots, sources, tensor):
    anywhere = pl.BlockSpec(memory_space=pl.ANY)
    flops = AUX_DEV * (MS * PA * BS * OCC * OCC * 4 + 2 * PA * OCC * (MS * BS) ** 2)
    return pl.pallas_call(
        main_kernel,
        out_shape=jax.ShapeDtypeStruct((DEVS * CAP * ROWS, LANES), jnp.bfloat16),
        grid_spec=pltpu.PrefetchScalarGridSpec(
            num_scalar_prefetch=2,
            grid=(AUX_DEV, PA // CHUNK),
            in_specs=[anywhere] * 7
            + [pl.BlockSpec((1, MS, CHUNK, BS, OCC), lambda p, c, *_: (p, 0, c, 0, 0))],
            out_specs=pl.BlockSpec((DEVS * CAP * ROWS, LANES), lambda p, c, *_: (0, 0)),
            scratch_shapes=[
                pltpu.VMEM((7 * BLK_DEV, BS, OCC), jnp.bfloat16),
                pltpu.VMEM((MS // 2, 2 * OCC, 2 * OCC), jnp.bfloat16),
                pltpu.VMEM((MS * BS, CHUNK * OCC), jnp.bfloat16),
                pltpu.VMEM((MS * BS, MS * BS), jnp.float32),
                pltpu.VMEM((DEVS * CAP, ROWS, LANES), jnp.float32),
                pltpu.SemaphoreType.DMA((7,)),
            ],
        ),
        compiler_params=pltpu.CompilerParams(
            dimension_semantics=("arbitrary", "arbitrary"), vmem_limit_bytes=40 * 1024 * 1024
        ),
        cost_estimate=pl.CostEstimate(flops=flops, bytes_accessed=22 * 1024 * 1024, transcendentals=0),
        name="products",
    )(picks, slots, *sources, tensor)


def collect_kernel(where, incoming, out, total):
    total[...] = jnp.zeros_like(total)
    for a in range(AUX):
        rows = incoming[pl.ds(a * ORB * CAP * ROWS, ORB * CAP * ROWS), :].astype(jnp.float32)
        summed = jnp.sum(rows.reshape(ORB, CAP * ROWS, LANES), axis=0)
        for k in range(CAP):
            total[where[a, k]] += summed[k * ROWS : (k + 1) * ROWS, :]
    for r in range(ROWS):
        line = total[:, r, :]
        for j in range(BS // ROWS):
            out[:, pl.ds((j * ROWS + r) * BS, BS)] = line[:, j * BS : (j + 1) * BS]


def collect(where, incoming):
    return pl.pallas_call(
        collect_kernel,
        out_shape=jax.ShapeDtypeStruct((OWN_DEV, BS * BS), jnp.float32),
        in_specs=[pl.BlockSpec(memory_space=pltpu.SMEM), pl.BlockSpec(memory_space=pltpu.VMEM)],
        out_specs=pl.BlockSpec(memory_space=pltpu.VMEM),
        scratch_shapes=[pltpu.VMEM((OWN_DEV, ROWS, LANES), jnp.float32)],
        compiler_params=pltpu.CompilerParams(vmem_limit_bytes=16 * 1024 * 1024),
        name="collect",
    )(where, incoming)


def body(three_center, orbitals, partners, pair_owner):
    aux, orb = lax.axis_index("aux"), lax.axis_index("orb")
    x, y = aux % SIDE, aux // SIDE
    even = orb % 2 == 0
    near, far = jnp.where(even, x, y), jnp.where(even, y, x)
    own = orbitals.reshape(BLK_DEV, BS, OCC)

    got = [lax.ppermute(own, AXES, shifted(-j, True)) for j in (1, 2, 3)]

    wanted = partners.reshape(ENTRIES)
    source = wanted // BLK_DEV
    source_x, source_y = source % SIDE, source // SIDE
    rel_near = (jnp.where(even, source_x, source_y) - near) % SIDE
    rel_far = (jnp.where(even, source_y, source_x) - far) % SIDE
    order = np.arange(ENTRIES)
    earlier = jnp.asarray(order[None, :] < order[:, None])
    rank = jnp.sum((rel_far[None, :] == rel_far[:, None]) & earlier, axis=1, dtype=jnp.int32)
    at_source = rel_near * BLK_DEV + wanted % BLK_DEV
    picks = jnp.where(rel_far == 0, at_source, SIDE * BLK_DEV + (rel_far - 1) * ROW_CAP + rank)

    table = pair_owner.reshape(E)
    lists = []
    for j in (1, 2, 3):
        hits = (rel_far[None, :] == j) & (rank[None, :] == jnp.arange(ROW_CAP, dtype=jnp.int32)[:, None])
        lists.append(jnp.sum(jnp.where(hits, at_source[None, :], 0), axis=1, dtype=jnp.int32))
    requests, tables = [], [table]
    for j in (1, 2, 3):
        sent = jnp.concatenate([lists[j - 1], table, jnp.zeros((384 - ROW_CAP - E,), jnp.int32)])
        there = lax.ppermute(sent.reshape(1, 384), AXES, shifted(j, False))
        requests.append(there[:, :LANES])
        tables.append(there[0, ROW_CAP : ROW_CAP + E])

    row_blocks = pack(requests, own, got)
    rows = [lax.ppermute(row_blocks[j - 1], AXES, shifted(-j, False)) for j in (1, 2, 3)]

    line = jnp.stack(tables)
    grid = [line] + [lax.ppermute(line, AXES, shifted(j, True)) for j in (1, 2, 3)]
    every = jnp.stack(grid)
    mine = every // OWN_DEV == aux * ORB + orb
    ranks = jnp.cumsum(mine.astype(jnp.int32), axis=2) - 1
    local = [
        jnp.sum(jnp.where(mine & (ranks == k), every % OWN_DEV, 0), axis=2, dtype=jnp.int32)
        for k in range(CAP)
    ]
    local = jnp.stack(local, axis=-1)
    steps = np.arange(SIDE)
    local = local[(near - steps) % SIDE][:, (far - steps) % SIDE]
    local = jnp.where(even, local.transpose(1, 0, 2), local).reshape(AUX, CAP)

    owner = table // OWN_DEV
    order = np.arange(E)
    earlier = jnp.asarray(order[None, :] < order[:, None])
    slots = owner * CAP + jnp.sum((owner[None, :] == owner[:, None]) & earlier, axis=1, dtype=jnp.int32)

    outgoing = products(picks, slots, (own, *got, *rows), three_center)
    incoming = lax.all_to_all(outgoing, AXES, split_axis=0, concat_axis=0, tiled=True)
    return collect(local, incoming)


def solution(mesh):
    in_specs = (
        P("aux", None, None, None, None),
        P("aux", "orb"),
        P("aux", None, None),
        P("aux", None),
    )
    out_specs = P(("aux", "orb"), None)
    return jax.shard_map(body, mesh=mesh, in_specs=in_specs, out_specs=out_specs, check_vma=False)
```

```python
import functools

import jax
import jax.numpy as jnp
import numpy as np
from jax import lax
from jax.experimental import pallas as pl
from jax.experimental.pallas import tpu as pltpu
from jax.sharding import PartitionSpec as P

BS = 32
PA = 64
MS = 8
NPS = 4
AUX_DEV = 4
NOCC = 1024
BLK_DEV = 64
OWN_DEV = 16
CAP = 3
FETCH = 16
EP = MS * (MS - 1)
E = AUX_DEV * EP
ENTRIES = AUX_DEV * MS * NPS
OCC = 128
SIDE = 4
AUX = SIDE * SIDE
ORB = 8
DEVS = AUX * ORB
ROW_CAP = SIDE * FETCH
EARLY = 32
LATE = ROW_CAP - EARLY
ROWS = 8
CHUNK = 8
LANES = 128
AXES = ("aux", "orb")


def shifted(step, near):
    pairs = []
    for aux in range(AUX):
        x, y = aux % SIDE, aux // SIDE
        for orb in range(ORB):
            if (orb % 2 == 0) == near:
                to = y * SIDE + (x + step) % SIDE
            else:
                to = ((y + step) % SIDE) * SIDE + x
            pairs.append((aux * ORB + orb, to * ORB + orb))
    return pairs


def in_vmem(array):
    return pltpu.with_memory_space_constraint(array, pltpu.VMEM)


def in_hbm(array):
    return pltpu.with_memory_space_constraint(array, pltpu.HBM)


VMEM = pl.BlockSpec(memory_space=pltpu.VMEM)
SMEM = pl.BlockSpec(memory_space=pltpu.SMEM)
HBM = pl.BlockSpec(memory_space=pltpu.HBM)
MIB = 1024 * 1024
LIST_ROW = AUX_DEV
BLOCKS = ROW_CAP + 3 * ROW_CAP
SOON = ROW_CAP + 3 * EARLY


def cost(flops, moved):
    return pl.CostEstimate(flops=flops, bytes_accessed=moved, transcendentals=0)


def columns(row):
    return jnp.broadcast_to(row, (LANES, LANES)).T


def plan_kernel(place, partners, owners, sent0, sent1, sent2, sent3, picks, slots, count):
    near, far, even = place[0], place[1], place[2]
    table = jnp.full((ROWS, LANES), -1, jnp.int32)
    for sent in (sent0, sent1, sent2, sent3):
        sent[...] = table
        sent[pl.ds(0, AUX_DEV), pl.ds(0, EP)] = owners[...]

    named = partners[...].reshape(AUX_DEV * MS, NPS)
    at = lax.broadcasted_iota(jnp.int32, (AUX_DEV * MS, LANES), 0) * NPS
    lane = lax.broadcasted_iota(jnp.int32, (AUX_DEV * MS, LANES), 1)
    spread = jnp.zeros((AUX_DEV * MS, LANES), jnp.int32)
    for k in range(NPS):
        spread += jnp.where(lane == at + k, named[:, k : k + 1], 0)
    wanted = jnp.sum(spread, axis=0, keepdims=True)

    down = lax.broadcasted_iota(jnp.int32, (LANES, LANES), 0)
    across = lax.broadcasted_iota(jnp.int32, (LANES, LANES), 1)
    earlier = down < across
    source, local = wanted >> 6, wanted & 63
    source_x, source_y = source & 3, source >> 2
    rel_near = (source_y + even * (source_x - source_y) - near) & 3
    rel_far = (source_x + even * (source_y - source_x) - far) & 3
    same = (columns(rel_far) == rel_far) & earlier
    rank = jnp.sum(same.astype(jnp.int32), axis=0, keepdims=True)
    packed = columns((rel_far * ROW_CAP + rank) * 256 + rel_near * BLK_DEV + local)
    key, value = packed >> 8, packed & 255
    for both, sends in enumerate(((sent0, sent1), (sent2, sent3))):
        line = jnp.sum(jnp.where(key == across + both * LANES, value, 0), axis=0, keepdims=True)
        for sent in sends:
            sent[pl.ds(LIST_ROW, 1), :] = line

    there = rel_far - 1
    remote = jnp.where(
        rank < EARLY, ROW_CAP + there * EARLY + rank, SOON + there * LATE + rank - EARLY
    )
    pick = jnp.where(rel_far == 0, rank, remote)
    picks[...] = pick
    missing = jnp.where(pick >= SOON, across[:1], LANES)
    count[...] = jnp.broadcast_to(jnp.min(missing, axis=1, keepdims=True) >> 5, (1, LANES))

    owner = sent0[...] >> 4
    stood = []
    for p in range(AUX_DEV):
        row = owner[p : p + 1]
        column = columns(row)
        hits = ((column == row) & earlier).astype(jnp.int32)
        for before in stood:
            hits += (before == row).astype(jnp.int32)
        slots[pl.ds(p, 1), :] = row * CAP + jnp.sum(hits, axis=0, keepdims=True)
        stood.append(column)


def plan(place, partners, owners):
    tile = jax.ShapeDtypeStruct((ROWS, LANES), jnp.int32)
    line = jax.ShapeDtypeStruct((1, LANES), jnp.int32)
    return pl.pallas_call(
        plan_kernel,
        out_shape=[tile] * 4 + [line, tile, line],
        in_specs=[SMEM] + [VMEM] * 2,
        out_specs=[VMEM] * 7,
        compiler_params=pltpu.CompilerParams(vmem_limit_bytes=2 * MIB),
        cost_estimate=cost(0, 64 * 1024),
        name="plan",
    )(place, partners, owners)


STAGED = (DEVS * CAP + 1, ROWS, LANES)
PAIRS = (2, MS // 2, 2 * OCC, 2 * OCC)


def stage_kernel(tensor, own, picks, slots, count, tensor_out, own_out, staged, pairs, sems):
    del picks, slots, count
    copies = [
        pltpu.make_async_copy(own, own_out, sems.at[0]),
        pltpu.make_async_copy(tensor, tensor_out, sems.at[1]),
    ]
    for copy in copies:
        copy.start()
    staged[...] = jnp.zeros_like(staged)
    pairs[...] = jnp.zeros_like(pairs)
    for copy in copies:
        copy.wait()


def stage(tensor, own, *lists):
    return pl.pallas_call(
        stage_kernel,
        out_shape=[
            pltpu.VMEM(tensor.shape, tensor.dtype),
            pltpu.VMEM(own.shape, own.dtype),
            pltpu.VMEM(STAGED, jnp.float32),
            pltpu.VMEM(PAIRS, jnp.bfloat16),
        ],
        in_specs=[HBM] * 2 + [SMEM] * 3,
        out_specs=[VMEM] * 4,
        scratch_shapes=[pltpu.SemaphoreType.DMA((2,))],
        compiler_params=pltpu.CompilerParams(vmem_limit_bytes=MIB),
        cost_estimate=cost(0, 18 * MIB),
        name="stage",
    )(in_hbm(tensor), in_hbm(own), *lists)


def pack_early_kernel(
    req1, req2, req3, own, got1, got2, got3, out1, out2, out3, shards
):
    for at, src in enumerate((own, got1, got2, got3)):
        shards[pl.ds(at * BLK_DEV, BLK_DEV)] = src[...]
    for j, (req, out) in enumerate(((req1, out1), (req2, out2), (req3, out3))):

        @pl.loop(0, EARLY, unroll=8)
        def _(r):
            out[r] = shards[req[LIST_ROW, (j + 1) % 2 * ROW_CAP + r]]


def block_array(rows):
    return pltpu.VMEM((rows, BS, OCC), jnp.bfloat16)


def pack_early(received, own, got):
    return pl.pallas_call(
        pack_early_kernel,
        out_shape=[block_array(EARLY)] * 3 + [block_array(SIDE * BLK_DEV)],
        in_specs=[SMEM] * 3 + [VMEM] * 4,
        out_specs=[VMEM] * 4,
        compiler_params=pltpu.CompilerParams(vmem_limit_bytes=2 * MIB),
        cost_estimate=cost(0, 4 * MIB),
        name="pack_early",
    )(*received, own, *[in_vmem(g) for g in got])


def pack_late_kernel(
    req0, req1, req2, req3, shards, mine, tab1, tab2, tab3, out0, out1, out2, out3, tables
):
    for at, src in enumerate((mine, tab1, tab2, tab3)):
        tables[at] = src[...]
    for j, (req, out) in enumerate(((req1, out1), (req2, out2), (req3, out3))):

        @pl.loop(0, LATE, unroll=8)
        def _(r):
            out[r] = shards[req[LIST_ROW, (j + 1) % 2 * ROW_CAP + EARLY + r]]

    @pl.loop(0, ROW_CAP, unroll=8)
    def _(r):
        out0[r] = shards[req0[LIST_ROW, r]]


def pack_late(mine, received, shards):
    return pl.pallas_call(
        pack_late_kernel,
        out_shape=[block_array(ROW_CAP)]
        + [block_array(LATE)] * 3
        + [pltpu.VMEM((SIDE, ROWS, LANES), jnp.int32)],
        in_specs=[SMEM] * 4 + [VMEM] * 5,
        out_specs=[VMEM] * 5,
        compiler_params=pltpu.CompilerParams(vmem_limit_bytes=2 * MIB),
        cost_estimate=cost(0, 2 * MIB),
        name="pack_late",
    )(mine, *received, shards, mine, *received)


def run_blocks(low, high, picks, slots, tensor, staged, pairs, blocks, total, half):
    def fill(p):
        for s in range(MS):
            side = (s % 2) * OCC
            for k in range(NPS):
                pairs[p % 2, s // 2, pl.ds(side + k * BS, BS), pl.ds(side, OCC)] = blocks[
                    picks[0, (p * MS + s) * NPS + k]
                ]

    def first(p, c):
        for pair in range(MS // 2):
            left = jnp.concatenate(
                [
                    tensor[p, 2 * pair + side, pl.ds(c * CHUNK, CHUNK)].reshape(CHUNK * BS, OCC)
                    for side in range(2)
                ],
                axis=1,
            )
            both = jnp.dot(left, pairs[p % 2, pair], preferred_element_type=jnp.float32)
            both = both.astype(jnp.bfloat16)
            for side in range(2):
                for a in range(CHUNK):
                    half[c % 2, pl.ds((2 * pair + side) * BS, BS), pl.ds(a * OCC, OCC)] = both[
                        a * BS : (a + 1) * BS, side * OCC : (side + 1) * OCC
                    ]

    def second(p, c):
        slab = half[c % 2]
        product = lax.dot_general(
            slab, slab, (((1,), (1,)), ((), ())), preferred_element_type=jnp.float32
        )
        if c == 0:
            total[p % 2] = product
        else:
            total[p % 2] += product

    @pl.when(low < high)
    def _():
        fill(low)

    last = PA // CHUNK

    @pl.loop(low, high)
    def _(p):
        first(p, 0)
        for c in range(last):
            if c + 1 < last:
                first(p, c + 1)
            second(p, c)
            if c == 0:
                put(jnp.maximum(p - 1, 0), p > 0, slots, total, staged)
            if c == 1:
                fill(jnp.minimum(p + 1, high - 1))


def put(p, valid, slots, total, staged):
    factor = np.float32(1.0 / np.sqrt(PA * NOCC))
    e = 0
    for s in range(MS):
        for t in range(MS):
            if s == t:
                continue
            tile = jnp.concatenate(
                [
                    total[p % 2, pl.ds(s * BS + j * ROWS, ROWS), pl.ds(t * BS, BS)]
                    for j in range(BS // ROWS)
                ],
                axis=1,
            )
            staged[jnp.where(valid, slots[p, e], DEVS * CAP)] = tile * factor
            e += 1


def early_kernel(
    count, picks, slots, row0, row1, row2, row3, tensor, staged0, pairs0,
    staged, pairs, blocks, total, half,
):
    del staged0, pairs0
    blocks[pl.ds(0, ROW_CAP)] = row0[...]
    for at, src in enumerate((row1, row2, row3)):
        blocks[pl.ds(ROW_CAP + at * EARLY, EARLY)] = src[...]
    run_blocks(0, count[0, 0], picks, slots, tensor, staged, pairs, blocks, total, half)


def late_kernel(
    count, picks, slots, late1, late2, late3, tensor, staged0, pairs0, blocks0, total0,
    staged, pairs, blocks, total, out, half,
):
    del staged0, pairs0, blocks0, total0
    for at, src in enumerate((late1, late2, late3)):
        blocks[pl.ds(SOON + at * LATE, LATE)] = src[...]
    run_blocks(count[0, 0], AUX_DEV, picks, slots, tensor, staged, pairs, blocks, total, half)
    put(AUX_DEV - 1, True, slots, total, staged)
    done = staged[pl.ds(0, DEVS * CAP)]
    out[...] = done.reshape(DEVS * CAP * ROWS, LANES).astype(jnp.bfloat16)


STATE = [
    pltpu.VMEM(STAGED, jnp.float32),
    pltpu.VMEM(PAIRS, jnp.bfloat16),
    pltpu.VMEM((BLOCKS, BS, OCC), jnp.bfloat16),
    pltpu.VMEM((2, MS * BS, MS * BS), jnp.float32),
]
HALF = pltpu.VMEM((2, MS * BS, CHUNK * OCC), jnp.bfloat16)
FLOPS = 2 * (MS * PA * BS * OCC * OCC * 4 + 2 * PA * OCC * (MS * BS) ** 2)


def early_products(count, picks, slots, rows, tensor, staged, pairs):
    return pl.pallas_call(
        early_kernel,
        out_shape=STATE,
        in_specs=[SMEM] * 3 + [VMEM] * 7,
        out_specs=[VMEM] * 4,
        input_output_aliases={8: 0, 9: 1},
        scratch_shapes=[HALF],
        compiler_params=pltpu.CompilerParams(vmem_limit_bytes=8 * MIB),
        cost_estimate=cost(FLOPS, 8 * MIB),
        name="early_products",
    )(count, picks, slots, *[in_vmem(r) for r in rows], tensor, staged, pairs)


def late_products(count, picks, slots, late, tensor, state):
    return pl.pallas_call(
        late_kernel,
        out_shape=STATE + [jax.ShapeDtypeStruct((DEVS * CAP * ROWS, LANES), jnp.bfloat16)],
        in_specs=[SMEM] * 3 + [VMEM] * 8,
        out_specs=[VMEM] * 5,
        input_output_aliases={7: 0, 8: 1, 9: 2, 10: 3},
        scratch_shapes=[HALF],
        compiler_params=pltpu.CompilerParams(vmem_limit_bytes=8 * MIB),
        cost_estimate=cost(FLOPS, 8 * MIB),
        name="late_products",
    )(count, picks, slots, *[in_vmem(r) for r in late], tensor, *state)[4]


def locate_kernel(place, tables0, tables1, tables2, tables3, where):
    none = 1 << 20
    lane = lax.broadcasted_iota(jnp.int32, (AUX, LANES), 1)
    left = []
    for p in range(AUX_DEV):
        row = jnp.concatenate(
            [tables[:, p, :] for tables in (tables0, tables1, tables2, tables3)], axis=0
        )
        mark = (p * LANES + lane) * OWN_DEV + (row & (OWN_DEV - 1))
        left.append(jnp.where((row >> 4) == place[3], mark, none))
    found = jnp.zeros((AUX, LANES), jnp.int32)
    for k in range(CAP):
        least = jnp.minimum(jnp.minimum(left[0], left[1]), jnp.minimum(left[2], left[3]))
        least = jnp.min(least, axis=1, keepdims=True)
        found = jnp.where(lane == k, least & (OWN_DEV - 1), found)
        left = [jnp.where(v > least, v, none) for v in left]
    where[...] = found


def locate(place, every):
    return pl.pallas_call(
        locate_kernel,
        out_shape=jax.ShapeDtypeStruct((AUX, LANES), jnp.int32),
        in_specs=[SMEM] + [VMEM] * 4,
        out_specs=VMEM,
        compiler_params=pltpu.CompilerParams(vmem_limit_bytes=2 * MIB),
        cost_estimate=cost(0, 64 * 1024),
        name="locate",
    )(place, *every)


def collect_kernel(place, where, incoming, out, total):
    total[...] = jnp.zeros_like(total)
    for a in range(AUX):
        x, y = a % SIDE, a // SIDE
        even = place[2] == 1
        i = (place[0] - jnp.where(even, x, y)) & 3
        j = (place[1] - jnp.where(even, y, x)) & 3
        rows = incoming[pl.ds(a * ORB * CAP * ROWS, ORB * CAP * ROWS), :].astype(jnp.float32)
        summed = jnp.sum(rows.reshape(ORB, CAP * ROWS, LANES), axis=0)
        for k in range(CAP):
            total[where[i * SIDE + j, k]] += summed[k * ROWS : (k + 1) * ROWS, :]
    for r in range(ROWS):
        line = total[:, r, :]
        for j in range(BS // ROWS):
            out[:, pl.ds((j * ROWS + r) * BS, BS)] = line[:, j * BS : (j + 1) * BS]


def collect(place, where, incoming):
    return pl.pallas_call(
        collect_kernel,
        out_shape=jax.ShapeDtypeStruct((OWN_DEV, BS * BS), jnp.float32),
        in_specs=[SMEM, SMEM, VMEM],
        out_specs=VMEM,
        scratch_shapes=[pltpu.VMEM((OWN_DEV, ROWS, LANES), jnp.float32)],
        compiler_params=pltpu.CompilerParams(vmem_limit_bytes=16 * MIB),
        name="collect",
    )(place, where, incoming)


def body(three_center, orbitals, partners, pair_owner):
    aux, orb = lax.axis_index("aux"), lax.axis_index("orb")
    x, y = aux % SIDE, aux // SIDE
    even = orb % 2 == 0
    near, far = jnp.where(even, x, y), jnp.where(even, y, x)
    own = orbitals.reshape(BLK_DEV, BS, OCC)

    got = [lax.ppermute(own, AXES, shifted(-j, True)) for j in (1, 2, 3)]

    place = jnp.stack([near, far, even.astype(jnp.int32), aux * ORB + orb]).astype(jnp.int32)
    mine, *sent, picks, slots, count = plan(place, partners, pair_owner)
    received = [lax.ppermute(sent[j - 1], AXES, shifted(j, False)) for j in (1, 2, 3)]

    tensor, own, staged, pairs = stage(three_center, own, picks, slots, count)
    *early, shards = pack_early(received, own, got)
    early = [lax.ppermute(early[j - 1], AXES, shifted(-j, False)) for j in (1, 2, 3)]
    row0, *late, tables = pack_late(mine, received, shards)
    late = [lax.ppermute(late[j - 1], AXES, shifted(-j, False)) for j in (1, 2, 3)]
    every = [tables] + [lax.ppermute(tables, AXES, shifted(j, True)) for j in (1, 2, 3)]

    state = early_products(count, picks, slots, (row0, *early), tensor, staged, pairs)
    outgoing = late_products(count, picks, slots, late, tensor, state)
    incoming = lax.all_to_all(outgoing, AXES, split_axis=0, concat_axis=0, tiled=True)

    return collect(place, locate(place, every), incoming)


def solution(mesh):
    in_specs = (
        P("aux", None, None, None, None),
        P("aux", "orb"),
        P("aux", None, None),
        P("aux", None),
    )
    out_specs = P(("aux", "orb"), None)
    return jax.shard_map(body, mesh=mesh, in_specs=in_specs, out_specs=out_specs, check_vma=False)
```

```python
import functools

import jax
import jax.numpy as jnp
import numpy as np
from jax import lax
from jax.experimental import pallas as pl
from jax.experimental.pallas import tpu as pltpu
from jax.sharding import PartitionSpec as P

BS = 32
PA = 64
MS = 8
NPS = 4
AUX_DEV = 4
NOCC = 1024
BLK_DEV = 64
OWN_DEV = 16
CAP = 3
FETCH = 16
EP = MS * (MS - 1)
E = AUX_DEV * EP
ENTRIES = AUX_DEV * MS * NPS
OCC = 128
SIDE = 4
AUX = SIDE * SIDE
ORB = 8
DEVS = AUX * ORB
ROW_CAP = SIDE * FETCH
EARLY = 32
LATE = ROW_CAP - EARLY
ROWS = 8
CHUNK = 8
LANES = 128
AXES = ("aux", "orb")


def shifted(step, near):
    pairs = []
    for aux in range(AUX):
        x, y = aux % SIDE, aux // SIDE
        for orb in range(ORB):
            if (orb % 2 == 0) == near:
                to = y * SIDE + (x + step) % SIDE
            else:
                to = ((y + step) % SIDE) * SIDE + x
            pairs.append((aux * ORB + orb, to * ORB + orb))
    return pairs


def in_vmem(array):
    return pltpu.with_memory_space_constraint(array, pltpu.VMEM)


def in_hbm(array):
    return pltpu.with_memory_space_constraint(array, pltpu.HBM)


VMEM = pl.BlockSpec(memory_space=pltpu.VMEM)
SMEM = pl.BlockSpec(memory_space=pltpu.SMEM)
HBM = pl.BlockSpec(memory_space=pltpu.HBM)
MIB = 1024 * 1024
LIST_ROW = AUX_DEV
BLOCKS = ROW_CAP + 3 * ROW_CAP
SOON = ROW_CAP + 3 * EARLY


def cost(flops, moved):
    return pl.CostEstimate(flops=flops, bytes_accessed=moved, transcendentals=0)


def columns(row):
    return jnp.broadcast_to(row, (LANES, LANES)).T


def plan_kernel(place, partners, owners, sent0, sent1, sent2, sent3, picks, slots, count):
    near, far, even = place[0], place[1], place[2]
    table = jnp.full((ROWS, LANES), -1, jnp.int32)
    for sent in (sent0, sent1, sent2, sent3):
        sent[...] = table
        sent[pl.ds(0, AUX_DEV), pl.ds(0, EP)] = owners[...]

    named = partners[...].reshape(AUX_DEV * MS, NPS)
    at = lax.broadcasted_iota(jnp.int32, (AUX_DEV * MS, LANES), 0) * NPS
    lane = lax.broadcasted_iota(jnp.int32, (AUX_DEV * MS, LANES), 1)
    spread = jnp.zeros((AUX_DEV * MS, LANES), jnp.int32)
    for k in range(NPS):
        spread += jnp.where(lane == at + k, named[:, k : k + 1], 0)
    wanted = jnp.sum(spread, axis=0, keepdims=True)

    down = lax.broadcasted_iota(jnp.int32, (LANES, LANES), 0)
    across = lax.broadcasted_iota(jnp.int32, (LANES, LANES), 1)
    earlier = down < across
    source, local = wanted >> 6, wanted & 63
    source_x, source_y = source & 3, source >> 2
    rel_near = (source_y + even * (source_x - source_y) - near) & 3
    rel_far = (source_x + even * (source_y - source_x) - far) & 3
    same = (columns(rel_far) == rel_far) & earlier
    rank = jnp.sum(same.astype(jnp.int32), axis=0, keepdims=True)
    packed = columns((rel_far * ROW_CAP + rank) * 256 + rel_near * BLK_DEV + local)
    key, value = packed >> 8, packed & 255
    for both, sends in enumerate(((sent0, sent1), (sent2, sent3))):
        line = jnp.sum(jnp.where(key == across + both * LANES, value, 0), axis=0, keepdims=True)
        for sent in sends:
            sent[pl.ds(LIST_ROW, 1), :] = line

    there = rel_far - 1
    remote = jnp.where(
        rank < EARLY, ROW_CAP + there * EARLY + rank, SOON + there * LATE + rank - EARLY
    )
    pick = jnp.where(rel_far == 0, rank, remote)
    picks[...] = pick
    missing = jnp.where(pick >= SOON, across[:1], LANES)
    count[...] = jnp.broadcast_to(jnp.min(missing, axis=1, keepdims=True) >> 5, (1, LANES))

    owner = sent0[...] >> 4
    stood = []
    for p in range(AUX_DEV):
        row = owner[p : p + 1]
        column = columns(row)
        hits = ((column == row) & earlier).astype(jnp.int32)
        for before in stood:
            hits += (before == row).astype(jnp.int32)
        slots[pl.ds(p, 1), :] = row * CAP + jnp.sum(hits, axis=0, keepdims=True)
        stood.append(column)


def plan(place, partners, owners):
    tile = jax.ShapeDtypeStruct((ROWS, LANES), jnp.int32)
    line = jax.ShapeDtypeStruct((1, LANES), jnp.int32)
    return pl.pallas_call(
        plan_kernel,
        out_shape=[tile] * 4 + [line, tile, line],
        in_specs=[SMEM] + [VMEM] * 2,
        out_specs=[VMEM] * 7,
        compiler_params=pltpu.CompilerParams(vmem_limit_bytes=2 * MIB),
        cost_estimate=cost(0, 64 * 1024),
        name="plan",
    )(place, partners, owners)


STAGED = (DEVS * CAP + 1, ROWS, LANES)
PAIRS = (2, MS // 2, 2 * OCC, 2 * OCC)


def stage_kernel(tensor, own, picks, slots, count, held, own_out, staged, pairs, sems):
    del picks, slots, count
    copies = [
        pltpu.make_async_copy(own, own_out, sems.at[0]),
        pltpu.make_async_copy(tensor.at[0], held.at[0], sems.at[1]),
    ]
    for copy in copies:
        copy.start()
    staged[...] = jnp.zeros_like(staged)
    pairs[...] = jnp.zeros_like(pairs)
    for copy in copies:
        copy.wait()


def stage(tensor, own, *lists):
    return pl.pallas_call(
        stage_kernel,
        out_shape=[
            pltpu.VMEM(tensor.shape, tensor.dtype),
            pltpu.VMEM(own.shape, own.dtype),
            pltpu.VMEM(STAGED, jnp.float32),
            pltpu.VMEM(PAIRS, jnp.bfloat16),
        ],
        in_specs=[HBM] * 2 + [SMEM] * 3,
        out_specs=[VMEM] * 4,
        scratch_shapes=[pltpu.SemaphoreType.DMA((2,))],
        compiler_params=pltpu.CompilerParams(vmem_limit_bytes=MIB),
        cost_estimate=cost(0, 5 * MIB),
        name="stage",
    )(in_hbm(tensor), in_hbm(own), *lists)


def pack_early_kernel(
    req1, req2, req3, own, got1, got2, got3, out1, out2, out3, shards
):
    for at, src in enumerate((own, got1, got2, got3)):
        shards[pl.ds(at * BLK_DEV, BLK_DEV)] = src[...]
    for j, (req, out) in enumerate(((req1, out1), (req2, out2), (req3, out3))):

        @pl.loop(0, EARLY, unroll=8)
        def _(r):
            out[r] = shards[req[LIST_ROW, (j + 1) % 2 * ROW_CAP + r]]


def block_array(rows):
    return pltpu.VMEM((rows, BS, OCC), jnp.bfloat16)


def pack_early(received, own, got):
    return pl.pallas_call(
        pack_early_kernel,
        out_shape=[block_array(EARLY)] * 3 + [block_array(SIDE * BLK_DEV)],
        in_specs=[SMEM] * 3 + [VMEM] * 4,
        out_specs=[VMEM] * 4,
        compiler_params=pltpu.CompilerParams(vmem_limit_bytes=2 * MIB),
        cost_estimate=cost(0, 4 * MIB),
        name="pack_early",
    )(*received, own, *[in_vmem(g) for g in got])


def pack_late_kernel(
    req0, req1, req2, req3, shards, mine, tab1, tab2, tab3, out0, out1, out2, out3, tables
):
    for at, src in enumerate((mine, tab1, tab2, tab3)):
        tables[at] = src[...]
    for j, (req, out) in enumerate(((req1, out1), (req2, out2), (req3, out3))):

        @pl.loop(0, LATE, unroll=8)
        def _(r):
            out[r] = shards[req[LIST_ROW, (j + 1) % 2 * ROW_CAP + EARLY + r]]

    @pl.loop(0, ROW_CAP, unroll=8)
    def _(r):
        out0[r] = shards[req0[LIST_ROW, r]]


def pack_late(mine, received, shards):
    return pl.pallas_call(
        pack_late_kernel,
        out_shape=[block_array(ROW_CAP)]
        + [block_array(LATE)] * 3
        + [
            pltpu.VMEM((SIDE, ROWS, LANES), jnp.int32),
        ],
        in_specs=[SMEM] * 4 + [VMEM] * 5,
        out_specs=[VMEM] * 5,
        compiler_params=pltpu.CompilerParams(vmem_limit_bytes=2 * MIB),
        cost_estimate=cost(0, 2 * MIB),
        name="pack_late",
    )(mine, *received, shards, mine, *received)


def run_blocks(low, high, picks, slots, tensor, staged, pairs, blocks, total, half, ready):
    def fill(p):
        for s in range(MS):
            side = (s % 2) * OCC
            for k in range(NPS):
                pairs[p % 2, s // 2, pl.ds(side + k * BS, BS), pl.ds(side, OCC)] = blocks[
                    picks[0, (p * MS + s) * NPS + k]
                ]

    def first(p, c):
        for pair in range(MS // 2):
            left = jnp.concatenate(
                [
                    tensor[p, 2 * pair + side, pl.ds(c * CHUNK, CHUNK)].reshape(CHUNK * BS, OCC)
                    for side in range(2)
                ],
                axis=1,
            )
            both = jnp.dot(left, pairs[p % 2, pair], preferred_element_type=jnp.float32)
            both = both.astype(jnp.bfloat16)
            for side in range(2):
                for a in range(CHUNK):
                    half[c % 2, pl.ds((2 * pair + side) * BS, BS), pl.ds(a * OCC, OCC)] = both[
                        a * BS : (a + 1) * BS, side * OCC : (side + 1) * OCC
                    ]

    def second(p, c):
        slab = half[c % 2]
        product = lax.dot_general(
            slab, slab, (((1,), (1,)), ((), ())), preferred_element_type=jnp.float32
        )
        if c == 0:
            total[p % 2] = product
        else:
            total[p % 2] += product

    @pl.when(low < high)
    def _():
        fill(low)

    last = PA // CHUNK

    @pl.loop(low, high)
    def _(p):
        ready(p)
        first(p, 0)
        for c in range(last):
            if c + 1 < last:
                first(p, c + 1)
            second(p, c)
            if c == 0:
                put(jnp.maximum(p - 1, 0), p > 0, slots, total, staged)
            if c == 1:
                fill(jnp.minimum(p + 1, high - 1))


def put(p, valid, slots, total, staged):
    factor = np.float32(1.0 / np.sqrt(PA * NOCC))
    e = 0
    for s in range(MS):
        for t in range(MS):
            if s == t:
                continue
            tile = jnp.concatenate(
                [
                    total[p % 2, pl.ds(s * BS + j * ROWS, ROWS), pl.ds(t * BS, BS)]
                    for j in range(BS // ROWS)
                ],
                axis=1,
            )
            staged[jnp.where(valid, slots[p, e], DEVS * CAP)] = tile * factor
            e += 1


def early_kernel(
    count, picks, slots, row0, row1, row2, row3, tensor, staged0, pairs0, held0,
    staged, pairs, held, blocks, total, half, sems,
):
    del staged0, pairs0, held0

    def rest(p):
        return pltpu.make_async_copy(tensor.at[p], held.at[p], sems.at[p])

    for p in range(1, AUX_DEV):
        rest(p).start()
    blocks[pl.ds(0, ROW_CAP)] = row0[...]
    for at, src in enumerate((row1, row2, row3)):
        blocks[pl.ds(ROW_CAP + at * EARLY, EARLY)] = src[...]

    def ready(p):
        @pl.when(p > 0)
        def _():
            rest(p).wait()

    run_blocks(0, count[0, 0], picks, slots, held, staged, pairs, blocks, total, half, ready)
    for p in range(1, AUX_DEV):

        @pl.when(p >= count[0, 0])
        def _():
            rest(p).wait()


def late_kernel(
    count, picks, slots, late1, late2, late3, staged0, pairs0, held0, blocks0, total0,
    staged, pairs, held, blocks, total, out, half,
):
    del staged0, pairs0, held0, blocks0, total0
    for at, src in enumerate((late1, late2, late3)):
        blocks[pl.ds(SOON + at * LATE, LATE)] = src[...]
    run_blocks(
        count[0, 0], AUX_DEV, picks, slots, held, staged, pairs, blocks, total, half, lambda p: None
    )
    put(AUX_DEV - 1, True, slots, total, staged)
    done = staged[pl.ds(0, DEVS * CAP)]
    out[...] = done.reshape(DEVS * CAP * ROWS, LANES).astype(jnp.bfloat16)


STATE = [
    pltpu.VMEM(STAGED, jnp.float32),
    pltpu.VMEM(PAIRS, jnp.bfloat16),
    pltpu.VMEM((AUX_DEV, MS, PA, BS, OCC), jnp.bfloat16),
    pltpu.VMEM((BLOCKS, BS, OCC), jnp.bfloat16),
    pltpu.VMEM((2, MS * BS, MS * BS), jnp.float32),
]
HALF = pltpu.VMEM((2, MS * BS, CHUNK * OCC), jnp.bfloat16)
FLOPS = 2 * (MS * PA * BS * OCC * OCC * 4 + 2 * PA * OCC * (MS * BS) ** 2)


def early_products(count, picks, slots, rows, tensor, staged, pairs, held):
    return pl.pallas_call(
        early_kernel,
        out_shape=STATE,
        in_specs=[SMEM] * 3 + [VMEM] * 4 + [HBM] + [VMEM] * 3,
        out_specs=[VMEM] * 5,
        input_output_aliases={8: 0, 9: 1, 10: 2},
        scratch_shapes=[HALF, pltpu.SemaphoreType.DMA((AUX_DEV,))],
        compiler_params=pltpu.CompilerParams(vmem_limit_bytes=8 * MIB),
        cost_estimate=cost(FLOPS, 8 * MIB),
        name="early_products",
    )(count, picks, slots, *[in_vmem(r) for r in rows], in_hbm(tensor), staged, pairs, held)


def late_products(count, picks, slots, late, state):
    return pl.pallas_call(
        late_kernel,
        out_shape=STATE + [jax.ShapeDtypeStruct((DEVS * CAP * ROWS, LANES), jnp.bfloat16)],
        in_specs=[SMEM] * 3 + [VMEM] * 8,
        out_specs=[VMEM] * 6,
        input_output_aliases={6: 0, 7: 1, 8: 2, 9: 3, 10: 4},
        scratch_shapes=[HALF],
        compiler_params=pltpu.CompilerParams(vmem_limit_bytes=8 * MIB),
        cost_estimate=cost(FLOPS, 8 * MIB),
        name="late_products",
    )(count, picks, slots, *[in_vmem(r) for r in late], *state)[5]


def locate_kernel(place, tables0, tables1, tables2, tables3, where):
    none = 1 << 20
    lane = lax.broadcasted_iota(jnp.int32, (AUX, LANES), 1)
    left = []
    for p in range(AUX_DEV):
        row = jnp.concatenate(
            [tables[:, p, :] for tables in (tables0, tables1, tables2, tables3)], axis=0
        )
        mark = (p * LANES + lane) * OWN_DEV + (row & (OWN_DEV - 1))
        left.append(jnp.where((row >> 4) == place[3], mark, none))
    found = jnp.zeros((AUX, LANES), jnp.int32)
    for k in range(CAP):
        least = jnp.minimum(jnp.minimum(left[0], left[1]), jnp.minimum(left[2], left[3]))
        least = jnp.min(least, axis=1, keepdims=True)
        found = jnp.where(lane == k, least & (OWN_DEV - 1), found)
        left = [jnp.where(v > least, v, none) for v in left]
    where[...] = found


def locate(place, every):
    return pl.pallas_call(
        locate_kernel,
        out_shape=jax.ShapeDtypeStruct((AUX, LANES), jnp.int32),
        in_specs=[SMEM] + [VMEM] * 4,
        out_specs=VMEM,
        compiler_params=pltpu.CompilerParams(vmem_limit_bytes=2 * MIB),
        cost_estimate=cost(0, 64 * 1024),
        name="locate",
    )(place, *every)


def collect_kernel(place, where, incoming, out, total):
    total[...] = jnp.zeros_like(total)
    for a in range(AUX):
        x, y = a % SIDE, a // SIDE
        even = place[2] == 1
        i = (place[0] - jnp.where(even, x, y)) & 3
        j = (place[1] - jnp.where(even, y, x)) & 3
        rows = incoming[pl.ds(a * ORB * CAP * ROWS, ORB * CAP * ROWS), :].astype(jnp.float32)
        summed = jnp.sum(rows.reshape(ORB, CAP * ROWS, LANES), axis=0)
        for k in range(CAP):
            total[where[i * SIDE + j, k]] += summed[k * ROWS : (k + 1) * ROWS, :]
    for r in range(ROWS):
        line = total[:, r, :]
        for j in range(BS // ROWS):
            out[:, pl.ds((j * ROWS + r) * BS, BS)] = line[:, j * BS : (j + 1) * BS]


def collect(place, where, incoming):
    return pl.pallas_call(
        collect_kernel,
        out_shape=jax.ShapeDtypeStruct((OWN_DEV, BS * BS), jnp.float32),
        in_specs=[SMEM, SMEM, VMEM],
        out_specs=VMEM,
        scratch_shapes=[pltpu.VMEM((OWN_DEV, ROWS, LANES), jnp.float32)],
        compiler_params=pltpu.CompilerParams(vmem_limit_bytes=16 * MIB),
        name="collect",
    )(place, where, incoming)


def body(three_center, orbitals, partners, pair_owner):
    aux, orb = lax.axis_index("aux"), lax.axis_index("orb")
    x, y = aux % SIDE, aux // SIDE
    even = orb % 2 == 0
    near, far = jnp.where(even, x, y), jnp.where(even, y, x)
    own = orbitals.reshape(BLK_DEV, BS, OCC)

    got = [lax.ppermute(own, AXES, shifted(-j, True)) for j in (1, 2, 3)]

    place = jnp.stack([near, far, even.astype(jnp.int32), aux * ORB + orb]).astype(jnp.int32)
    mine, *sent, picks, slots, count = plan(place, partners, pair_owner)
    received = [lax.ppermute(sent[j - 1], AXES, shifted(j, False)) for j in (1, 2, 3)]

    held, here, staged, pairs = stage(three_center, own, picks, slots, count)
    *early, shards = pack_early(received, here, got)
    early = [lax.ppermute(early[j - 1], AXES, shifted(-j, False)) for j in (1, 2, 3)]
    row0, *late, tables = pack_late(mine, received, shards)
    late = [lax.ppermute(late[j - 1], AXES, shifted(-j, False)) for j in (1, 2, 3)]
    every = [tables] + [lax.ppermute(tables, AXES, shifted(j, True)) for j in (1, 2, 3)]

    state = early_products(
        count, picks, slots, (row0, *early), three_center, staged, pairs, held
    )
    outgoing = late_products(count, picks, slots, late, state)
    incoming = lax.all_to_all(outgoing, AXES, split_axis=0, concat_axis=0, tiled=True)

    return collect(place, locate(place, every), incoming)


def solution(mesh):
    in_specs = (
        P("aux", None, None, None, None),
        P("aux", "orb"),
        P("aux", None, None),
        P("aux", None),
    )
    out_specs = P(("aux", "orb"), None)
    return jax.shard_map(body, mesh=mesh, in_specs=in_specs, out_specs=out_specs, check_vma=False)
```

```python
import functools

import jax
import jax.numpy as jnp
import numpy as np
from jax import lax
from jax.experimental import pallas as pl
from jax.experimental.pallas import tpu as pltpu
from jax.sharding import PartitionSpec as P

BS = 32
PA = 64
MS = 8
NPS = 4
AUX_DEV = 4
NOCC = 1024
BLK_DEV = 64
OWN_DEV = 16
CAP = 3
FETCH = 16
EP = MS * (MS - 1)
E = AUX_DEV * EP
ENTRIES = AUX_DEV * MS * NPS
OCC = 128
SIDE = 4
AUX = SIDE * SIDE
ORB = 8
DEVS = AUX * ORB
ROW_CAP = SIDE * FETCH
EARLY = 32
LATE = ROW_CAP - EARLY
ROWS = 8
CHUNK = 8
LANES = 128
AXES = ("aux", "orb")


def shifted(step, near):
    pairs = []
    for aux in range(AUX):
        x, y = aux % SIDE, aux // SIDE
        for orb in range(ORB):
            if (orb % 2 == 0) == near:
                to = y * SIDE + (x + step) % SIDE
            else:
                to = ((y + step) % SIDE) * SIDE + x
            pairs.append((aux * ORB + orb, to * ORB + orb))
    return pairs


def in_vmem(array):
    return pltpu.with_memory_space_constraint(array, pltpu.VMEM)


def in_hbm(array):
    return pltpu.with_memory_space_constraint(array, pltpu.HBM)


VMEM = pl.BlockSpec(memory_space=pltpu.VMEM)
SMEM = pl.BlockSpec(memory_space=pltpu.SMEM)
HBM = pl.BlockSpec(memory_space=pltpu.HBM)
MIB = 1024 * 1024
LIST_ROW = AUX_DEV
SIDE_SLOTS = DEVS * CAP // 2
BLOCKS = ROW_CAP + 3 * ROW_CAP
SOON = ROW_CAP + 3 * EARLY


def cost(flops, moved):
    return pl.CostEstimate(flops=flops, bytes_accessed=moved, transcendentals=0)


def columns(row):
    return jnp.broadcast_to(row, (LANES, LANES)).T


def plan_kernel(place, partners, owners, sent0, sent1, sent2, sent3, picks, slots, count):
    near, far, even = place[0], place[1], place[2]
    table = jnp.full((ROWS, LANES), -1, jnp.int32)
    for sent in (sent0, sent1, sent2, sent3):
        sent[...] = table
        sent[pl.ds(0, AUX_DEV), pl.ds(0, EP)] = owners[...]

    named = partners[...].reshape(AUX_DEV * MS, NPS)
    at = lax.broadcasted_iota(jnp.int32, (AUX_DEV * MS, LANES), 0) * NPS
    lane = lax.broadcasted_iota(jnp.int32, (AUX_DEV * MS, LANES), 1)
    spread = jnp.zeros((AUX_DEV * MS, LANES), jnp.int32)
    for k in range(NPS):
        spread += jnp.where(lane == at + k, named[:, k : k + 1], 0)
    wanted = jnp.sum(spread, axis=0, keepdims=True)

    down = lax.broadcasted_iota(jnp.int32, (LANES, LANES), 0)
    across = lax.broadcasted_iota(jnp.int32, (LANES, LANES), 1)
    earlier = down < across
    source, local = wanted >> 6, wanted & 63
    source_x, source_y = source & 3, source >> 2
    rel_near = (source_y + even * (source_x - source_y) - near) & 3
    rel_far = (source_x + even * (source_y - source_x) - far) & 3
    same = (columns(rel_far) == rel_far) & earlier
    rank = jnp.sum(same.astype(jnp.int32), axis=0, keepdims=True)
    packed = columns((rel_far * ROW_CAP + rank) * 256 + rel_near * BLK_DEV + local)
    key, value = packed >> 8, packed & 255
    for both, sends in enumerate(((sent0, sent1), (sent2, sent3))):
        line = jnp.sum(jnp.where(key == across + both * LANES, value, 0), axis=0, keepdims=True)
        for sent in sends:
            sent[pl.ds(LIST_ROW, 1), :] = line

    there = rel_far - 1
    remote = jnp.where(
        rank < EARLY, ROW_CAP + there * EARLY + rank, SOON + there * LATE + rank - EARLY
    )
    pick = jnp.where(rel_far == 0, rank, remote)
    picks[...] = pick
    missing = jnp.where(pick >= SOON, across[:1], LANES)
    count[...] = jnp.broadcast_to(jnp.min(missing, axis=1, keepdims=True) >> 5, (1, LANES))

    owner = sent0[...] >> 4
    stood = []
    for p in range(AUX_DEV):
        row = owner[p : p + 1]
        column = columns(row)
        hits = ((column == row) & earlier).astype(jnp.int32)
        for before in stood:
            hits += (before == row).astype(jnp.int32)
        at = (row & 1) * SIDE_SLOTS + (row >> 1) * CAP
        slots[pl.ds(p, 1), :] = at + jnp.sum(hits, axis=0, keepdims=True)
        stood.append(column)


def plan(place, partners, owners):
    tile = jax.ShapeDtypeStruct((ROWS, LANES), jnp.int32)
    line = jax.ShapeDtypeStruct((1, LANES), jnp.int32)
    return pl.pallas_call(
        plan_kernel,
        out_shape=[tile] * 4 + [line, tile, line],
        in_specs=[SMEM] + [VMEM] * 2,
        out_specs=[VMEM] * 7,
        compiler_params=pltpu.CompilerParams(vmem_limit_bytes=2 * MIB),
        cost_estimate=cost(0, 64 * 1024),
        name="plan",
    )(place, partners, owners)


STAGED = (DEVS * CAP + 1, ROWS, LANES)
PAIRS = (2, MS // 2, 2 * OCC, 2 * OCC)


def stage_kernel(tensor, own, picks, slots, count, held, own_out, staged, pairs, sems):
    del picks, slots, count
    copies = [
        pltpu.make_async_copy(own, own_out, sems.at[0]),
        pltpu.make_async_copy(tensor.at[0], held.at[0], sems.at[1]),
    ]
    for copy in copies:
        copy.start()
    staged[...] = jnp.zeros_like(staged)
    pairs[...] = jnp.zeros_like(pairs)
    for copy in copies:
        copy.wait()


def stage(tensor, own, *lists):
    return pl.pallas_call(
        stage_kernel,
        out_shape=[
            pltpu.VMEM(tensor.shape, tensor.dtype),
            pltpu.VMEM(own.shape, own.dtype),
            pltpu.VMEM(STAGED, jnp.float32),
            pltpu.VMEM(PAIRS, jnp.bfloat16),
        ],
        in_specs=[HBM] * 2 + [SMEM] * 3,
        out_specs=[VMEM] * 4,
        scratch_shapes=[pltpu.SemaphoreType.DMA((2,))],
        compiler_params=pltpu.CompilerParams(vmem_limit_bytes=MIB),
        cost_estimate=cost(0, 5 * MIB),
        name="stage",
    )(in_hbm(tensor), in_hbm(own), *lists)


def pack_early_kernel(
    req1, req2, req3, own, got1, got2, got3, out1, out2, out3, shards
):
    for at, src in enumerate((own, got1, got2, got3)):
        shards[pl.ds(at * BLK_DEV, BLK_DEV)] = src[...]
    for j, (req, out) in enumerate(((req1, out1), (req2, out2), (req3, out3))):

        @pl.loop(0, EARLY, unroll=8)
        def _(r):
            out[r] = shards[req[LIST_ROW, (j + 1) % 2 * ROW_CAP + r]]


def block_array(rows):
    return pltpu.VMEM((rows, BS, OCC), jnp.bfloat16)


def pack_early(received, own, got):
    return pl.pallas_call(
        pack_early_kernel,
        out_shape=[block_array(EARLY)] * 3 + [block_array(SIDE * BLK_DEV)],
        in_specs=[SMEM] * 3 + [VMEM] * 4,
        out_specs=[VMEM] * 4,
        compiler_params=pltpu.CompilerParams(vmem_limit_bytes=2 * MIB),
        cost_estimate=cost(0, 4 * MIB),
        name="pack_early",
    )(*received, own, *[in_vmem(g) for g in got])


def pack_late_kernel(
    req0, req1, req2, req3, shards, mine, tab1, tab2, tab3, out0, out1, out2, out3, tables
):
    for at, src in enumerate((mine, tab1, tab2, tab3)):
        tables[at] = src[...]
    for j, (req, out) in enumerate(((req1, out1), (req2, out2), (req3, out3))):

        @pl.loop(0, LATE, unroll=8)
        def _(r):
            out[r] = shards[req[LIST_ROW, (j + 1) % 2 * ROW_CAP + EARLY + r]]

    @pl.loop(0, ROW_CAP, unroll=8)
    def _(r):
        out0[r] = shards[req0[LIST_ROW, r]]


def pack_late(mine, received, shards):
    return pl.pallas_call(
        pack_late_kernel,
        out_shape=[block_array(ROW_CAP)]
        + [block_array(LATE)] * 3
        + [
            pltpu.VMEM((SIDE, ROWS, LANES), jnp.int32),
        ],
        in_specs=[SMEM] * 4 + [VMEM] * 5,
        out_specs=[VMEM] * 5,
        compiler_params=pltpu.CompilerParams(vmem_limit_bytes=2 * MIB),
        cost_estimate=cost(0, 2 * MIB),
        name="pack_late",
    )(mine, *received, shards, mine, *received)


def run_blocks(low, high, picks, slots, tensor, staged, pairs, blocks, total, half, ready):
    def fill(p):
        for s in range(MS):
            side = (s % 2) * OCC
            for k in range(NPS):
                pairs[p % 2, s // 2, pl.ds(side + k * BS, BS), pl.ds(side, OCC)] = blocks[
                    picks[0, (p * MS + s) * NPS + k]
                ]

    def first(p, c):
        for pair in range(MS // 2):
            left = jnp.concatenate(
                [
                    tensor[p, 2 * pair + side, pl.ds(c * CHUNK, CHUNK)].reshape(CHUNK * BS, OCC)
                    for side in range(2)
                ],
                axis=1,
            )
            both = jnp.dot(left, pairs[p % 2, pair], preferred_element_type=jnp.float32)
            both = both.astype(jnp.bfloat16)
            for side in range(2):
                for a in range(CHUNK):
                    half[c % 2, pl.ds((2 * pair + side) * BS, BS), pl.ds(a * OCC, OCC)] = both[
                        a * BS : (a + 1) * BS, side * OCC : (side + 1) * OCC
                    ]

    def second(p, c):
        slab = half[c % 2]
        product = lax.dot_general(
            slab, slab, (((1,), (1,)), ((), ())), preferred_element_type=jnp.float32
        )
        if c == 0:
            total[p % 2] = product
        else:
            total[p % 2] += product

    @pl.when(low < high)
    def _():
        fill(low)

    last = PA // CHUNK

    @pl.loop(low, high)
    def _(p):
        ready(p)
        first(p, 0)
        for c in range(last):
            if c + 1 < last:
                first(p, c + 1)
            second(p, c)
            if c == 0:
                put(jnp.maximum(p - 1, 0), p > 0, slots, total, staged)
            if c == 1:
                fill(jnp.minimum(p + 1, high - 1))


def put(p, valid, slots, total, staged):
    factor = np.float32(1.0 / np.sqrt(PA * NOCC))
    e = 0
    for s in range(MS):
        for t in range(MS):
            if s == t:
                continue
            tile = jnp.concatenate(
                [
                    total[p % 2, pl.ds(s * BS + j * ROWS, ROWS), pl.ds(t * BS, BS)]
                    for j in range(BS // ROWS)
                ],
                axis=1,
            )
            staged[jnp.where(valid, slots[p, e], DEVS * CAP)] = tile * factor
            e += 1


def early_kernel(
    count, picks, slots, row0, row1, row2, row3, tensor, staged0, pairs0, held0,
    staged, pairs, held, blocks, total, half, sems,
):
    del staged0, pairs0, held0

    def rest(p):
        return pltpu.make_async_copy(tensor.at[p], held.at[p], sems.at[p])

    for p in range(1, AUX_DEV):
        rest(p).start()
    blocks[pl.ds(0, ROW_CAP)] = row0[...]
    for at, src in enumerate((row1, row2, row3)):
        blocks[pl.ds(ROW_CAP + at * EARLY, EARLY)] = src[...]

    def ready(p):
        @pl.when(p > 0)
        def _():
            rest(p).wait()

    run_blocks(0, count[0, 0], picks, slots, held, staged, pairs, blocks, total, half, ready)
    for p in range(1, AUX_DEV):

        @pl.when(p >= count[0, 0])
        def _():
            rest(p).wait()


def late_kernel(
    place, count, picks, slots, late1, late2, late3, staged0, pairs0, held0, blocks0, total0,
    staged, pairs, held, blocks, total, out, half,
):
    del staged0, pairs0, held0, blocks0, total0
    for at, src in enumerate((late1, late2, late3)):
        blocks[pl.ds(SOON + at * LATE, LATE)] = src[...]
    run_blocks(
        count[0, 0], AUX_DEV, picks, slots, held, staged, pairs, blocks, total, half, lambda p: None
    )
    put(AUX_DEV - 1, True, slots, total, staged)
    done = staged[pl.ds(place[2] * SIDE_SLOTS, SIDE_SLOTS)]
    out[...] = done.reshape(SIDE_SLOTS * ROWS, LANES).astype(jnp.bfloat16)


def join_kernel(place, staged, came, out):
    kept = staged[pl.ds((1 - place[2]) * SIDE_SLOTS, SIDE_SLOTS)].reshape(SIDE_SLOTS * ROWS, LANES)
    out[...] = (kept + came[...].astype(jnp.float32)).astype(jnp.bfloat16)


def join(place, staged, came):
    return pl.pallas_call(
        join_kernel,
        out_shape=jax.ShapeDtypeStruct(came.shape, came.dtype),
        in_specs=[SMEM] + [VMEM] * 2,
        out_specs=VMEM,
        compiler_params=pltpu.CompilerParams(vmem_limit_bytes=4 * MIB),
        cost_estimate=cost(0, 2 * MIB),
        name="join",
    )(place, staged, in_vmem(came))


STATE = [
    pltpu.VMEM(STAGED, jnp.float32),
    pltpu.VMEM(PAIRS, jnp.bfloat16),
    pltpu.VMEM((AUX_DEV, MS, PA, BS, OCC), jnp.bfloat16),
    pltpu.VMEM((BLOCKS, BS, OCC), jnp.bfloat16),
    pltpu.VMEM((2, MS * BS, MS * BS), jnp.float32),
]
HALF = pltpu.VMEM((2, MS * BS, CHUNK * OCC), jnp.bfloat16)
FLOPS = 2 * (MS * PA * BS * OCC * OCC * 4 + 2 * PA * OCC * (MS * BS) ** 2)


def early_products(count, picks, slots, rows, tensor, staged, pairs, held):
    return pl.pallas_call(
        early_kernel,
        out_shape=STATE,
        in_specs=[SMEM] * 3 + [VMEM] * 4 + [HBM] + [VMEM] * 3,
        out_specs=[VMEM] * 5,
        input_output_aliases={8: 0, 9: 1, 10: 2},
        scratch_shapes=[HALF, pltpu.SemaphoreType.DMA((AUX_DEV,))],
        compiler_params=pltpu.CompilerParams(vmem_limit_bytes=8 * MIB),
        cost_estimate=cost(FLOPS, 8 * MIB),
        name="early_products",
    )(count, picks, slots, *[in_vmem(r) for r in rows], in_hbm(tensor), staged, pairs, held)


def late_products(place, count, picks, slots, late, state):
    return pl.pallas_call(
        late_kernel,
        out_shape=STATE + [jax.ShapeDtypeStruct((SIDE_SLOTS * ROWS, LANES), jnp.bfloat16)],
        in_specs=[SMEM] * 4 + [VMEM] * 8,
        out_specs=[VMEM] * 6,
        input_output_aliases={7: 0, 8: 1, 9: 2, 10: 3, 11: 4},
        scratch_shapes=[HALF],
        compiler_params=pltpu.CompilerParams(vmem_limit_bytes=8 * MIB),
        cost_estimate=cost(FLOPS, 8 * MIB),
        name="late_products",
    )(place, count, picks, slots, *[in_vmem(r) for r in late], *state)


def locate_kernel(place, tables0, tables1, tables2, tables3, where):
    none = 1 << 20
    lane = lax.broadcasted_iota(jnp.int32, (AUX, LANES), 1)
    left = []
    for p in range(AUX_DEV):
        row = jnp.concatenate(
            [tables[:, p, :] for tables in (tables0, tables1, tables2, tables3)], axis=0
        )
        mark = (p * LANES + lane) * OWN_DEV + (row & (OWN_DEV - 1))
        left.append(jnp.where((row >> 4) == place[3], mark, none))
    found = jnp.zeros((AUX, LANES), jnp.int32)
    for k in range(CAP):
        least = jnp.minimum(jnp.minimum(left[0], left[1]), jnp.minimum(left[2], left[3]))
        least = jnp.min(least, axis=1, keepdims=True)
        found = jnp.where(lane == k, least & (OWN_DEV - 1), found)
        left = [jnp.where(v > least, v, none) for v in left]
    where[...] = found


def locate(place, every):
    return pl.pallas_call(
        locate_kernel,
        out_shape=jax.ShapeDtypeStruct((AUX, LANES), jnp.int32),
        in_specs=[SMEM] + [VMEM] * 4,
        out_specs=VMEM,
        compiler_params=pltpu.CompilerParams(vmem_limit_bytes=2 * MIB),
        cost_estimate=cost(0, 64 * 1024),
        name="locate",
    )(place, *every)


def collect_kernel(place, where, incoming, out, total):
    total[...] = jnp.zeros_like(total)
    for a in range(AUX):
        x, y = a % SIDE, a // SIDE
        even = place[2] == 1
        i = (place[0] - jnp.where(even, x, y)) & 3
        j = (place[1] - jnp.where(even, y, x)) & 3
        rows = incoming[pl.ds(a * SIDE * CAP * ROWS, SIDE * CAP * ROWS), :].astype(jnp.float32)
        summed = jnp.sum(rows.reshape(SIDE, CAP * ROWS, LANES), axis=0)
        for k in range(CAP):
            total[where[i * SIDE + j, k]] += summed[k * ROWS : (k + 1) * ROWS, :]
    for r in range(ROWS):
        line = total[:, r, :]
        for j in range(BS // ROWS):
            out[:, pl.ds((j * ROWS + r) * BS, BS)] = line[:, j * BS : (j + 1) * BS]


def collect(place, where, incoming):
    return pl.pallas_call(
        collect_kernel,
        out_shape=jax.ShapeDtypeStruct((OWN_DEV, BS * BS), jnp.float32),
        in_specs=[SMEM, SMEM, VMEM],
        out_specs=VMEM,
        scratch_shapes=[pltpu.VMEM((OWN_DEV, ROWS, LANES), jnp.float32)],
        compiler_params=pltpu.CompilerParams(vmem_limit_bytes=16 * MIB),
        name="collect",
    )(place, where, incoming)


def body(three_center, orbitals, partners, pair_owner):
    aux, orb = lax.axis_index("aux"), lax.axis_index("orb")
    x, y = aux % SIDE, aux // SIDE
    even = orb % 2 == 0
    near, far = jnp.where(even, x, y), jnp.where(even, y, x)
    own = orbitals.reshape(BLK_DEV, BS, OCC)

    got = [lax.ppermute(own, AXES, shifted(-j, True)) for j in (1, 2, 3)]

    place = jnp.stack([near, far, even.astype(jnp.int32), aux * ORB + orb]).astype(jnp.int32)
    mine, *sent, picks, slots, count = plan(place, partners, pair_owner)
    received = [lax.ppermute(sent[j - 1], AXES, shifted(j, False)) for j in (1, 2, 3)]

    held, here, staged, pairs = stage(three_center, own, picks, slots, count)
    *early, shards = pack_early(received, here, got)
    early = [lax.ppermute(early[j - 1], AXES, shifted(-j, False)) for j in (1, 2, 3)]
    row0, *late, tables = pack_late(mine, received, shards)
    late = [lax.ppermute(late[j - 1], AXES, shifted(-j, False)) for j in (1, 2, 3)]
    every = [tables] + [lax.ppermute(tables, AXES, shifted(j, True)) for j in (1, 2, 3)]

    state = early_products(
        count, picks, slots, (row0, *early), three_center, staged, pairs, held
    )
    state = late_products(place, count, picks, slots, late, state)
    swap = [(device, device ^ 1) for device in range(DEVS)]
    outgoing = join(place, state[0], lax.ppermute(state[5], AXES, swap))
    cores = [list(range(core, DEVS, 2)) for core in range(2)]
    incoming = lax.all_to_all(
        outgoing, AXES, split_axis=0, concat_axis=0, axis_index_groups=cores, tiled=True
    )

    return collect(place, locate(place, every), incoming)


def solution(mesh):
    in_specs = (
        P("aux", None, None, None, None),
        P("aux", "orb"),
        P("aux", None, None),
        P("aux", None),
    )
    out_specs = P(("aux", "orb"), None)
    return jax.shard_map(body, mesh=mesh, in_specs=in_specs, out_specs=out_specs, check_vma=False)
```

```python
import functools

import jax
import jax.numpy as jnp
import numpy as np
from jax import lax
from jax.experimental import pallas as pl
from jax.experimental.pallas import tpu as pltpu
from jax.sharding import PartitionSpec as P

BS = 32
PA = 64
MS = 8
NPS = 4
AUX_DEV = 4
NOCC = 1024
BLK_DEV = 64
OWN_DEV = 16
CAP = 3
FETCH = 16
EP = MS * (MS - 1)
E = AUX_DEV * EP
ENTRIES = AUX_DEV * MS * NPS
OCC = 128
SIDE = 4
AUX = SIDE * SIDE
ORB = 8
DEVS = AUX * ORB
ROW_CAP = SIDE * FETCH
EARLY = 32
LATE = ROW_CAP - EARLY
ROWS = 8
CHUNK = 8
LANES = 128
AXES = ("aux", "orb")


def shifted(step, near):
    pairs = []
    for aux in range(AUX):
        x, y = aux % SIDE, aux // SIDE
        for orb in range(ORB):
            if (orb % 2 == 0) == near:
                to = y * SIDE + (x + step) % SIDE
            else:
                to = ((y + step) % SIDE) * SIDE + x
            pairs.append((aux * ORB + orb, to * ORB + orb))
    return pairs


def in_vmem(array):
    return pltpu.with_memory_space_constraint(array, pltpu.VMEM)


def in_hbm(array):
    return pltpu.with_memory_space_constraint(array, pltpu.HBM)


VMEM = pl.BlockSpec(memory_space=pltpu.VMEM)
SMEM = pl.BlockSpec(memory_space=pltpu.SMEM)
HBM = pl.BlockSpec(memory_space=pltpu.HBM)
MIB = 1024 * 1024
LIST_ROW = AUX_DEV
PICKS, COUNT, EVEN = 4, 5, 6
SIDE_SLOTS = DEVS * CAP // 2
BLOCKS = ROW_CAP + 3 * ROW_CAP
SOON = ROW_CAP + 3 * EARLY


def cost(flops, moved):
    return pl.CostEstimate(flops=flops, bytes_accessed=moved, transcendentals=0)


def columns(row):
    return jnp.broadcast_to(row, (LANES, LANES)).T


def plan_kernel(place, partners, owners, sent0, sent1, sent2, sent3, lists):
    near, far, even = place[0], place[1], place[2]
    table = jnp.full((ROWS, LANES), -1, jnp.int32)
    for sent in (sent0, sent1, sent2, sent3):
        sent[...] = table
        sent[pl.ds(0, AUX_DEV), pl.ds(0, EP)] = owners[...]

    named = partners[...].reshape(AUX_DEV * MS, NPS)
    at = lax.broadcasted_iota(jnp.int32, (AUX_DEV * MS, LANES), 0) * NPS
    lane = lax.broadcasted_iota(jnp.int32, (AUX_DEV * MS, LANES), 1)
    spread = jnp.zeros((AUX_DEV * MS, LANES), jnp.int32)
    for k in range(NPS):
        spread += jnp.where(lane == at + k, named[:, k : k + 1], 0)
    wanted = jnp.sum(spread, axis=0, keepdims=True)

    down = lax.broadcasted_iota(jnp.int32, (LANES, LANES), 0)
    across = lax.broadcasted_iota(jnp.int32, (LANES, LANES), 1)
    earlier = down < across
    source, local = wanted >> 6, wanted & 63
    source_x, source_y = source & 3, source >> 2
    rel_near = (source_y + even * (source_x - source_y) - near) & 3
    rel_far = (source_x + even * (source_y - source_x) - far) & 3
    same = (columns(rel_far) == rel_far) & earlier
    rank = jnp.sum(same.astype(jnp.int32), axis=0, keepdims=True)
    packed = columns((rel_far * ROW_CAP + rank) * 256 + rel_near * BLK_DEV + local)
    key, value = packed >> 8, packed & 255
    for both, sends in enumerate(((sent0, sent1), (sent2, sent3))):
        line = jnp.sum(jnp.where(key == across + both * LANES, value, 0), axis=0, keepdims=True)
        for sent in sends:
            sent[pl.ds(LIST_ROW, 1), :] = line

    there = rel_far - 1
    remote = jnp.where(
        rank < EARLY, ROW_CAP + there * EARLY + rank, SOON + there * LATE + rank - EARLY
    )
    pick = jnp.where(rel_far == 0, rank, remote)
    lists[pl.ds(PICKS, 1), :] = pick
    missing = jnp.where(pick >= SOON, across[:1], LANES)
    count = jnp.min(missing, axis=1, keepdims=True) >> 5
    lists[pl.ds(COUNT, 1), :] = jnp.broadcast_to(count, (1, LANES))
    lists[pl.ds(EVEN, 2), :] = jnp.broadcast_to(even, (2, LANES))

    owner = sent0[...] >> 4
    stood = []
    for p in range(AUX_DEV):
        row = owner[p : p + 1]
        column = columns(row)
        hits = ((column == row) & earlier).astype(jnp.int32)
        for before in stood:
            hits += (before == row).astype(jnp.int32)
        at = (row & 1) * SIDE_SLOTS + (row >> 1) * CAP
        lists[pl.ds(p, 1), :] = at + jnp.sum(hits, axis=0, keepdims=True)
        stood.append(column)


def plan(place, partners, owners):
    tile = jax.ShapeDtypeStruct((ROWS, LANES), jnp.int32)
    return pl.pallas_call(
        plan_kernel,
        out_shape=[tile] * 5,
        in_specs=[SMEM] + [VMEM] * 2,
        out_specs=[VMEM] * 5,
        compiler_params=pltpu.CompilerParams(vmem_limit_bytes=2 * MIB),
        cost_estimate=cost(0, 64 * 1024),
        name="plan",
    )(place, partners, owners)


STAGED = (DEVS * CAP + 1, ROWS, LANES)
PAIRS = (2, MS // 2, 2 * OCC, 2 * OCC)


def stage_kernel(tensor, own, lists, held, own_out, staged, pairs, sems):
    del lists
    copies = [
        pltpu.make_async_copy(own, own_out, sems.at[0]),
        pltpu.make_async_copy(tensor.at[0], held.at[0], sems.at[1]),
    ]
    for copy in copies:
        copy.start()
    staged[...] = jnp.zeros_like(staged)
    pairs[...] = jnp.zeros_like(pairs)
    for copy in copies:
        copy.wait()


def stage(tensor, own, lists):
    return pl.pallas_call(
        stage_kernel,
        out_shape=[
            pltpu.VMEM(tensor.shape, tensor.dtype),
            pltpu.VMEM(own.shape, own.dtype),
            pltpu.VMEM(STAGED, jnp.float32),
            pltpu.VMEM(PAIRS, jnp.bfloat16),
        ],
        in_specs=[HBM] * 2 + [SMEM],
        out_specs=[VMEM] * 4,
        scratch_shapes=[pltpu.SemaphoreType.DMA((2,))],
        compiler_params=pltpu.CompilerParams(vmem_limit_bytes=MIB),
        cost_estimate=cost(0, 5 * MIB),
        name="stage",
    )(in_hbm(tensor), in_hbm(own), lists)


def pack_early_kernel(
    req1, req2, req3, own, got1, got2, got3, out1, out2, out3, shards
):
    for at, src in enumerate((own, got1, got2, got3)):
        shards[pl.ds(at * BLK_DEV, BLK_DEV)] = src[...]
    for j, (req, out) in enumerate(((req1, out1), (req2, out2), (req3, out3))):

        @pl.loop(0, EARLY, unroll=8)
        def _(r):
            out[r] = shards[req[LIST_ROW, (j + 1) % 2 * ROW_CAP + r]]


def block_array(rows):
    return pltpu.VMEM((rows, BS, OCC), jnp.bfloat16)


def pack_early(received, own, got):
    return pl.pallas_call(
        pack_early_kernel,
        out_shape=[block_array(EARLY)] * 3 + [block_array(SIDE * BLK_DEV)],
        in_specs=[SMEM] * 3 + [VMEM] * 4,
        out_specs=[VMEM] * 4,
        compiler_params=pltpu.CompilerParams(vmem_limit_bytes=2 * MIB),
        cost_estimate=cost(0, 4 * MIB),
        name="pack_early",
    )(*received, own, *[in_vmem(g) for g in got])


def pack_late_kernel(
    req0, req1, req2, req3, shards, mine, tab1, tab2, tab3, out0, out1, out2, out3, tables
):
    for at, src in enumerate((mine, tab1, tab2, tab3)):
        tables[at] = src[...]
    for j, (req, out) in enumerate(((req1, out1), (req2, out2), (req3, out3))):

        @pl.loop(0, LATE, unroll=8)
        def _(r):
            out[r] = shards[req[LIST_ROW, (j + 1) % 2 * ROW_CAP + EARLY + r]]

    @pl.loop(0, ROW_CAP, unroll=8)
    def _(r):
        out0[r] = shards[req0[LIST_ROW, r]]


def pack_late(mine, received, shards):
    return pl.pallas_call(
        pack_late_kernel,
        out_shape=[block_array(ROW_CAP)]
        + [block_array(LATE)] * 3
        + [
            pltpu.VMEM((SIDE, ROWS, LANES), jnp.int32),
        ],
        in_specs=[SMEM] * 4 + [VMEM] * 5,
        out_specs=[VMEM] * 5,
        compiler_params=pltpu.CompilerParams(vmem_limit_bytes=2 * MIB),
        cost_estimate=cost(0, 2 * MIB),
        name="pack_late",
    )(mine, *received, shards, mine, *received)


def run_blocks(low, high, lists, tensor, staged, pairs, blocks, total, half, ready):
    def fill(p):
        for s in range(MS):
            side = (s % 2) * OCC
            for k in range(NPS):
                pairs[p % 2, s // 2, pl.ds(side + k * BS, BS), pl.ds(side, OCC)] = blocks[
                    lists[PICKS, (p * MS + s) * NPS + k]
                ]

    def first(p, c):
        for pair in range(MS // 2):
            left = jnp.concatenate(
                [
                    tensor[p, 2 * pair + side, pl.ds(c * CHUNK, CHUNK)].reshape(CHUNK * BS, OCC)
                    for side in range(2)
                ],
                axis=1,
            )
            both = jnp.dot(left, pairs[p % 2, pair], preferred_element_type=jnp.float32)
            both = both.astype(jnp.bfloat16)
            for side in range(2):
                for a in range(CHUNK):
                    half[c % 2, pl.ds((2 * pair + side) * BS, BS), pl.ds(a * OCC, OCC)] = both[
                        a * BS : (a + 1) * BS, side * OCC : (side + 1) * OCC
                    ]

    def second(p, c):
        slab = half[c % 2]
        product = lax.dot_general(
            slab, slab, (((1,), (1,)), ((), ())), preferred_element_type=jnp.float32
        )
        if c == 0:
            total[p % 2] = product
        else:
            total[p % 2] += product

    @pl.when(low < high)
    def _():
        fill(low)

    last = PA // CHUNK

    @pl.loop(low, high)
    def _(p):
        ready(p)
        first(p, 0)
        for c in range(last):
            if c + 1 < last:
                first(p, c + 1)
            second(p, c)
            if c == 0:
                put(jnp.maximum(p - 1, 0), p > 0, lists, total, staged)
            if c == 1:
                fill(jnp.minimum(p + 1, high - 1))


def put(p, valid, lists, total, staged):
    factor = np.float32(1.0 / np.sqrt(PA * NOCC))
    e = 0
    for s in range(MS):
        for t in range(MS):
            if s == t:
                continue
            tile = jnp.concatenate(
                [
                    total[p % 2, pl.ds(s * BS + j * ROWS, ROWS), pl.ds(t * BS, BS)]
                    for j in range(BS // ROWS)
                ],
                axis=1,
            )
            staged[jnp.where(valid, lists[p, e], DEVS * CAP)] = tile * factor
            e += 1


def early_kernel(
    lists, row0, row1, row2, row3, tensor, staged0, pairs0, held0,
    staged, pairs, held, blocks, total, half, sems,
):
    del staged0, pairs0, held0

    def rest(p):
        return pltpu.make_async_copy(tensor.at[p], held.at[p], sems.at[p])

    for p in range(1, AUX_DEV):
        rest(p).start()
    blocks[pl.ds(0, ROW_CAP)] = row0[...]
    for at, src in enumerate((row1, row2, row3)):
        blocks[pl.ds(ROW_CAP + at * EARLY, EARLY)] = src[...]

    def ready(p):
        @pl.when(p > 0)
        def _():
            rest(p).wait()

    run_blocks(0, lists[COUNT, 0], lists, held, staged, pairs, blocks, total, half, ready)
    for p in range(1, AUX_DEV):

        @pl.when(p >= lists[COUNT, 0])
        def _():
            rest(p).wait()


def late_kernel(
    lists, late1, late2, late3, staged0, pairs0, held0, blocks0, total0,
    staged, pairs, held, blocks, total, out, half,
):
    del staged0, pairs0, held0, blocks0, total0
    for at, src in enumerate((late1, late2, late3)):
        blocks[pl.ds(SOON + at * LATE, LATE)] = src[...]
    run_blocks(
        lists[COUNT, 0], AUX_DEV, lists, held, staged, pairs, blocks, total, half, lambda p: None
    )
    put(AUX_DEV - 1, True, lists, total, staged)
    done = staged[pl.ds(lists[EVEN, 0] * SIDE_SLOTS, SIDE_SLOTS)]
    out[...] = done.reshape(SIDE_SLOTS * ROWS, LANES).astype(jnp.bfloat16)


def join_kernel(lists, staged, came, out):
    kept = staged[pl.ds((1 - lists[EVEN, 0]) * SIDE_SLOTS, SIDE_SLOTS)].reshape(SIDE_SLOTS * ROWS, LANES)
    out[...] = (kept + came[...].astype(jnp.float32)).astype(jnp.bfloat16)


def join(lists, staged, came):
    return pl.pallas_call(
        join_kernel,
        out_shape=jax.ShapeDtypeStruct(came.shape, came.dtype),
        in_specs=[SMEM] + [VMEM] * 2,
        out_specs=VMEM,
        compiler_params=pltpu.CompilerParams(vmem_limit_bytes=4 * MIB),
        cost_estimate=cost(0, 2 * MIB),
        name="join",
    )(lists, staged, in_vmem(came))


STATE = [
    pltpu.VMEM(STAGED, jnp.float32),
    pltpu.VMEM(PAIRS, jnp.bfloat16),
    pltpu.VMEM((AUX_DEV, MS, PA, BS, OCC), jnp.bfloat16),
    pltpu.VMEM((BLOCKS, BS, OCC), jnp.bfloat16),
    pltpu.VMEM((2, MS * BS, MS * BS), jnp.float32),
]
HALF = pltpu.VMEM((2, MS * BS, CHUNK * OCC), jnp.bfloat16)
FLOPS = 2 * (MS * PA * BS * OCC * OCC * 4 + 2 * PA * OCC * (MS * BS) ** 2)


def early_products(lists, rows, tensor, staged, pairs, held):
    return pl.pallas_call(
        early_kernel,
        out_shape=STATE,
        in_specs=[SMEM] + [VMEM] * 4 + [HBM] + [VMEM] * 3,
        out_specs=[VMEM] * 5,
        input_output_aliases={6: 0, 7: 1, 8: 2},
        scratch_shapes=[HALF, pltpu.SemaphoreType.DMA((AUX_DEV,))],
        compiler_params=pltpu.CompilerParams(vmem_limit_bytes=8 * MIB),
        cost_estimate=cost(FLOPS, 8 * MIB),
        name="early_products",
    )(lists, *[in_vmem(r) for r in rows], in_hbm(tensor), staged, pairs, held)


def late_products(lists, late, state):
    return pl.pallas_call(
        late_kernel,
        out_shape=STATE + [jax.ShapeDtypeStruct((SIDE_SLOTS * ROWS, LANES), jnp.bfloat16)],
        in_specs=[SMEM] + [VMEM] * 8,
        out_specs=[VMEM] * 6,
        input_output_aliases={4: 0, 5: 1, 6: 2, 7: 3, 8: 4},
        scratch_shapes=[HALF],
        compiler_params=pltpu.CompilerParams(vmem_limit_bytes=8 * MIB),
        cost_estimate=cost(FLOPS, 8 * MIB),
        name="late_products",
    )(lists, *[in_vmem(r) for r in late], *state)


def locate_kernel(place, tables0, tables1, tables2, tables3, where):
    none = 1 << 20
    lane = lax.broadcasted_iota(jnp.int32, (AUX, LANES), 1)
    left = []
    for p in range(AUX_DEV):
        row = jnp.concatenate(
            [tables[:, p, :] for tables in (tables0, tables1, tables2, tables3)], axis=0
        )
        mark = (p * LANES + lane) * OWN_DEV + (row & (OWN_DEV - 1))
        left.append(jnp.where((row >> 4) == place[3], mark, none))
    found = jnp.zeros((AUX, LANES), jnp.int32)
    for k in range(CAP):
        least = jnp.minimum(jnp.minimum(left[0], left[1]), jnp.minimum(left[2], left[3]))
        least = jnp.min(least, axis=1, keepdims=True)
        found = jnp.where(lane == k, least & (OWN_DEV - 1), found)
        left = [jnp.where(v > least, v, none) for v in left]
    where[...] = found


def locate(place, every):
    return pl.pallas_call(
        locate_kernel,
        out_shape=jax.ShapeDtypeStruct((AUX, LANES), jnp.int32),
        in_specs=[SMEM] + [VMEM] * 4,
        out_specs=VMEM,
        compiler_params=pltpu.CompilerParams(vmem_limit_bytes=2 * MIB),
        cost_estimate=cost(0, 64 * 1024),
        name="locate",
    )(place, *every)


def collect_kernel(place, where, incoming, out, total):
    total[...] = jnp.zeros_like(total)
    for a in range(AUX):
        x, y = a % SIDE, a // SIDE
        even = place[2] == 1
        i = (place[0] - jnp.where(even, x, y)) & 3
        j = (place[1] - jnp.where(even, y, x)) & 3
        rows = incoming[pl.ds(a * SIDE * CAP * ROWS, SIDE * CAP * ROWS), :].astype(jnp.float32)
        summed = jnp.sum(rows.reshape(SIDE, CAP * ROWS, LANES), axis=0)
        for k in range(CAP):
            total[where[i * SIDE + j, k]] += summed[k * ROWS : (k + 1) * ROWS, :]
    for r in range(ROWS):
        line = total[:, r, :]
        for j in range(BS // ROWS):
            out[:, pl.ds((j * ROWS + r) * BS, BS)] = line[:, j * BS : (j + 1) * BS]


def collect(place, where, incoming):
    return pl.pallas_call(
        collect_kernel,
        out_shape=jax.ShapeDtypeStruct((OWN_DEV, BS * BS), jnp.float32),
        in_specs=[SMEM, SMEM, VMEM],
        out_specs=VMEM,
        scratch_shapes=[pltpu.VMEM((OWN_DEV, ROWS, LANES), jnp.float32)],
        compiler_params=pltpu.CompilerParams(vmem_limit_bytes=16 * MIB),
        name="collect",
    )(place, where, incoming)


def body(three_center, orbitals, partners, pair_owner):
    aux, orb = lax.axis_index("aux"), lax.axis_index("orb")
    x, y = aux % SIDE, aux // SIDE
    even = orb % 2 == 0
    near, far = jnp.where(even, x, y), jnp.where(even, y, x)
    own = orbitals.reshape(BLK_DEV, BS, OCC)

    got = [lax.ppermute(own, AXES, shifted(-j, True)) for j in (1, 2, 3)]

    place = jnp.stack([near, far, even.astype(jnp.int32), aux * ORB + orb]).astype(jnp.int32)
    mine, *sent, lists = plan(place, partners, pair_owner)
    received = [lax.ppermute(sent[j - 1], AXES, shifted(j, False)) for j in (1, 2, 3)]

    held, here, staged, pairs = stage(three_center, own, lists)
    *early, shards = pack_early(received, here, got)
    early = [lax.ppermute(early[j - 1], AXES, shifted(-j, False)) for j in (1, 2, 3)]
    row0, *late, tables = pack_late(mine, received, shards)
    late = [lax.ppermute(late[j - 1], AXES, shifted(-j, False)) for j in (1, 2, 3)]
    every = [tables] + [lax.ppermute(tables, AXES, shifted(j, True)) for j in (1, 2, 3)]

    state = early_products(
        lists, (row0, *early), three_center, staged, pairs, held
    )
    state = late_products(lists, late, state)
    swap = [(device, device ^ 1) for device in range(DEVS)]
    outgoing = join(lists, state[0], lax.ppermute(state[5], AXES, swap))
    cores = [list(range(core, DEVS, 2)) for core in range(2)]
    incoming = lax.all_to_all(
        outgoing, AXES, split_axis=0, concat_axis=0, axis_index_groups=cores, tiled=True
    )

    return collect(place, locate(place, every), incoming)


def solution(mesh):
    in_specs = (
        P("aux", None, None, None, None),
        P("aux", "orb"),
        P("aux", None, None),
        P("aux", None),
    )
    out_specs = P(("aux", "orb"), None)
    return jax.shard_map(body, mesh=mesh, in_specs=in_specs, out_specs=out_specs, check_vma=False)
```

```python
import functools

import jax
import jax.numpy as jnp
import numpy as np
from jax import lax
from jax.experimental import pallas as pl
from jax.experimental.pallas import tpu as pltpu
from jax.sharding import PartitionSpec as P

BS = 32
PA = 64
MS = 8
NPS = 4
AUX_DEV = 4
NOCC = 1024
BLK_DEV = 64
OWN_DEV = 16
CAP = 3
FETCH = 16
EP = MS * (MS - 1)
E = AUX_DEV * EP
ENTRIES = AUX_DEV * MS * NPS
OCC = 128
SIDE = 4
AUX = SIDE * SIDE
ORB = 8
DEVS = AUX * ORB
ROW_CAP = SIDE * FETCH
EARLY = 32
LATE = ROW_CAP - EARLY
ROWS = 8
CHUNK = 8
LANES = 128
AXES = ("aux", "orb")


def shifted(step, near):
    pairs = []
    for aux in range(AUX):
        x, y = aux % SIDE, aux // SIDE
        for orb in range(ORB):
            if (orb % 2 == 0) == near:
                to = y * SIDE + (x + step) % SIDE
            else:
                to = ((y + step) % SIDE) * SIDE + x
            pairs.append((aux * ORB + orb, to * ORB + orb))
    return pairs


def in_vmem(array):
    return pltpu.with_memory_space_constraint(array, pltpu.VMEM)


def in_hbm(array):
    return pltpu.with_memory_space_constraint(array, pltpu.HBM)


VMEM = pl.BlockSpec(memory_space=pltpu.VMEM)
SMEM = pl.BlockSpec(memory_space=pltpu.SMEM)
HBM = pl.BlockSpec(memory_space=pltpu.HBM)
MIB = 1024 * 1024
LIST_ROW = AUX_DEV
SIDE_SLOTS = DEVS * CAP // 2
BLOCKS = ROW_CAP + 3 * ROW_CAP
SOON = ROW_CAP + 3 * EARLY


def cost(flops, moved):
    return pl.CostEstimate(flops=flops, bytes_accessed=moved, transcendentals=0)


def columns(row):
    return jnp.broadcast_to(row, (LANES, LANES)).T


def plan_kernel(place, partners, owners, sent0, sent1, sent2, sent3, picks, slots, count):
    near, far, even = place[0], place[1], place[2]
    table = jnp.full((ROWS, LANES), -1, jnp.int32)
    for sent in (sent0, sent1, sent2, sent3):
        sent[...] = table
        sent[pl.ds(0, AUX_DEV), pl.ds(0, EP)] = owners[...]

    named = partners[...].reshape(AUX_DEV * MS, NPS)
    at = lax.broadcasted_iota(jnp.int32, (AUX_DEV * MS, LANES), 0) * NPS
    lane = lax.broadcasted_iota(jnp.int32, (AUX_DEV * MS, LANES), 1)
    spread = jnp.zeros((AUX_DEV * MS, LANES), jnp.int32)
    for k in range(NPS):
        spread += jnp.where(lane == at + k, named[:, k : k + 1], 0)
    wanted = jnp.sum(spread, axis=0, keepdims=True)

    down = lax.broadcasted_iota(jnp.int32, (LANES, LANES), 0)
    across = lax.broadcasted_iota(jnp.int32, (LANES, LANES), 1)
    earlier = down < across
    source, local = wanted >> 6, wanted & 63
    source_x, source_y = source & 3, source >> 2
    rel_near = (source_y + even * (source_x - source_y) - near) & 3
    rel_far = (source_x + even * (source_y - source_x) - far) & 3
    same = (columns(rel_far) == rel_far) & earlier
    rank = jnp.sum(same.astype(jnp.int32), axis=0, keepdims=True)
    packed = columns((rel_far * ROW_CAP + rank) * 256 + rel_near * BLK_DEV + local)
    key, value = packed >> 8, packed & 255
    for both, sends in enumerate(((sent0, sent1), (sent2, sent3))):
        line = jnp.sum(jnp.where(key == across + both * LANES, value, 0), axis=0, keepdims=True)
        for sent in sends:
            sent[pl.ds(LIST_ROW, 1), :] = line

    there = rel_far - 1
    remote = jnp.where(
        rank < EARLY, ROW_CAP + there * EARLY + rank, SOON + there * LATE + rank - EARLY
    )
    pick = jnp.where(rel_far == 0, rank, remote)
    picks[...] = pick
    missing = jnp.where(pick >= SOON, across[:1], LANES)
    count[...] = jnp.broadcast_to(jnp.min(missing, axis=1, keepdims=True) >> 5, (1, LANES))

    owner = sent0[...] >> 4
    stood = []
    for p in range(AUX_DEV):
        row = owner[p : p + 1]
        column = columns(row)
        hits = ((column == row) & earlier).astype(jnp.int32)
        for before in stood:
            hits += (before == row).astype(jnp.int32)
        at = (row & 1) * SIDE_SLOTS + (row >> 1) * CAP
        slots[pl.ds(p, 1), :] = at + jnp.sum(hits, axis=0, keepdims=True)
        stood.append(column)


def plan(place, partners, owners):
    tile = jax.ShapeDtypeStruct((ROWS, LANES), jnp.int32)
    line = jax.ShapeDtypeStruct((1, LANES), jnp.int32)
    return pl.pallas_call(
        plan_kernel,
        out_shape=[tile] * 4 + [line, tile, line],
        in_specs=[SMEM] + [VMEM] * 2,
        out_specs=[VMEM] * 7,
        compiler_params=pltpu.CompilerParams(vmem_limit_bytes=2 * MIB),
        cost_estimate=cost(0, 64 * 1024),
        name="plan",
    )(place, partners, owners)


STAGED = (DEVS * CAP + 1, ROWS, LANES)
PAIRS = (2, MS // 2, 2 * OCC, 2 * OCC)


def stage_kernel(own, count, own_out, sem):
    del count
    copy = pltpu.make_async_copy(own, own_out, sem)
    copy.start()
    copy.wait()


def stage(own, count):
    return pl.pallas_call(
        stage_kernel,
        out_shape=pltpu.VMEM(own.shape, own.dtype),
        in_specs=[HBM, VMEM],
        out_specs=VMEM,
        scratch_shapes=[pltpu.SemaphoreType.DMA],
        compiler_params=pltpu.CompilerParams(vmem_limit_bytes=MIB),
        cost_estimate=cost(0, MIB),
        name="stage",
    )(in_hbm(own), count)


def head_kernel(tensor, after, held, staged, pairs, sem):
    del after
    copy = pltpu.make_async_copy(tensor.at[0], held.at[0], sem)
    copy.start()
    staged[...] = jnp.zeros_like(staged)
    pairs[...] = jnp.zeros_like(pairs)
    copy.wait()


def head(tensor, after):
    return pl.pallas_call(
        head_kernel,
        out_shape=[
            pltpu.VMEM(tensor.shape, tensor.dtype),
            pltpu.VMEM(STAGED, jnp.float32),
            pltpu.VMEM(PAIRS, jnp.bfloat16),
        ],
        in_specs=[HBM, VMEM],
        out_specs=[VMEM] * 3,
        scratch_shapes=[pltpu.SemaphoreType.DMA],
        compiler_params=pltpu.CompilerParams(vmem_limit_bytes=MIB),
        cost_estimate=cost(0, 5 * MIB),
        name="head",
    )(in_hbm(tensor), in_vmem(after))


def pack_early_kernel(
    req1, req2, req3, own, got1, got2, got3, out1, out2, out3, shards
):
    for at, src in enumerate((own, got1, got2, got3)):
        shards[pl.ds(at * BLK_DEV, BLK_DEV)] = src[...]
    for j, (req, out) in enumerate(((req1, out1), (req2, out2), (req3, out3))):

        @pl.loop(0, EARLY, unroll=8)
        def _(r):
            out[r] = shards[req[LIST_ROW, (j + 1) % 2 * ROW_CAP + r]]


def block_array(rows):
    return pltpu.VMEM((rows, BS, OCC), jnp.bfloat16)


def pack_early(received, own, got):
    return pl.pallas_call(
        pack_early_kernel,
        out_shape=[block_array(EARLY)] * 3 + [block_array(SIDE * BLK_DEV)],
        in_specs=[SMEM] * 3 + [VMEM] * 4,
        out_specs=[VMEM] * 4,
        compiler_params=pltpu.CompilerParams(vmem_limit_bytes=2 * MIB),
        cost_estimate=cost(0, 4 * MIB),
        name="pack_early",
    )(*received, own, *[in_vmem(g) for g in got])


def pack_late_kernel(
    req0, req1, req2, req3, shards, mine, tab1, tab2, tab3, out0, out1, out2, out3, tables
):
    for at, src in enumerate((mine, tab1, tab2, tab3)):
        tables[at] = src[...]
    for j, (req, out) in enumerate(((req1, out1), (req2, out2), (req3, out3))):

        @pl.loop(0, LATE, unroll=8)
        def _(r):
            out[r] = shards[req[LIST_ROW, (j + 1) % 2 * ROW_CAP + EARLY + r]]

    @pl.loop(0, ROW_CAP, unroll=8)
    def _(r):
        out0[r] = shards[req0[LIST_ROW, r]]


def pack_late(mine, received, shards):
    return pl.pallas_call(
        pack_late_kernel,
        out_shape=[block_array(ROW_CAP)]
        + [block_array(LATE)] * 3
        + [
            pltpu.VMEM((SIDE, ROWS, LANES), jnp.int32),
        ],
        in_specs=[SMEM] * 4 + [VMEM] * 5,
        out_specs=[VMEM] * 5,
        compiler_params=pltpu.CompilerParams(vmem_limit_bytes=2 * MIB),
        cost_estimate=cost(0, 2 * MIB),
        name="pack_late",
    )(mine, *received, shards, mine, *received)


def run_blocks(low, high, picks, slots, tensor, staged, pairs, blocks, total, half, ready):
    def fill(p):
        for s in range(MS):
            side = (s % 2) * OCC
            for k in range(NPS):
                pairs[p % 2, s // 2, pl.ds(side + k * BS, BS), pl.ds(side, OCC)] = blocks[
                    picks[0, (p * MS + s) * NPS + k]
                ]

    def first(p, c):
        for pair in range(MS // 2):
            left = jnp.concatenate(
                [
                    tensor[p, 2 * pair + side, pl.ds(c * CHUNK, CHUNK)].reshape(CHUNK * BS, OCC)
                    for side in range(2)
                ],
                axis=1,
            )
            both = jnp.dot(left, pairs[p % 2, pair], preferred_element_type=jnp.float32)
            both = both.astype(jnp.bfloat16)
            for side in range(2):
                for a in range(CHUNK):
                    half[c % 2, pl.ds((2 * pair + side) * BS, BS), pl.ds(a * OCC, OCC)] = both[
                        a * BS : (a + 1) * BS, side * OCC : (side + 1) * OCC
                    ]

    def second(p, c):
        slab = half[c % 2]
        product = lax.dot_general(
            slab, slab, (((1,), (1,)), ((), ())), preferred_element_type=jnp.float32
        )
        if c == 0:
            total[p % 2] = product
        else:
            total[p % 2] += product

    @pl.when(low < high)
    def _():
        fill(low)

    last = PA // CHUNK

    @pl.loop(low, high)
    def _(p):
        ready(p)
        first(p, 0)
        for c in range(last):
            if c + 1 < last:
                first(p, c + 1)
            second(p, c)
            if c == 0:
                put(jnp.maximum(p - 1, 0), p > 0, slots, total, staged)
            if c == 1:
                fill(jnp.minimum(p + 1, high - 1))


def put(p, valid, slots, total, staged):
    factor = np.float32(1.0 / np.sqrt(PA * NOCC))
    e = 0
    for s in range(MS):
        for t in range(MS):
            if s == t:
                continue
            tile = jnp.concatenate(
                [
                    total[p % 2, pl.ds(s * BS + j * ROWS, ROWS), pl.ds(t * BS, BS)]
                    for j in range(BS // ROWS)
                ],
                axis=1,
            )
            staged[jnp.where(valid, slots[p, e], DEVS * CAP)] = tile * factor
            e += 1


def early_kernel(
    count, picks, slots, row0, row1, row2, row3, tensor, staged0, pairs0, held0,
    staged, pairs, held, blocks, total, half, sems,
):
    del staged0, pairs0, held0

    def rest(p):
        return pltpu.make_async_copy(tensor.at[p], held.at[p], sems.at[p])

    for p in range(1, AUX_DEV):
        rest(p).start()
    blocks[pl.ds(0, ROW_CAP)] = row0[...]
    for at, src in enumerate((row1, row2, row3)):
        blocks[pl.ds(ROW_CAP + at * EARLY, EARLY)] = src[...]

    def ready(p):
        @pl.when(p > 0)
        def _():
            rest(p).wait()

    run_blocks(0, count[0, 0], picks, slots, held, staged, pairs, blocks, total, half, ready)
    for p in range(1, AUX_DEV):

        @pl.when(p >= count[0, 0])
        def _():
            rest(p).wait()


def late_kernel(
    place, count, picks, slots, late1, late2, late3, staged0, pairs0, held0, blocks0, total0,
    staged, pairs, held, blocks, total, out, half,
):
    del staged0, pairs0, held0, blocks0, total0
    for at, src in enumerate((late1, late2, late3)):
        blocks[pl.ds(SOON + at * LATE, LATE)] = src[...]
    run_blocks(
        count[0, 0], AUX_DEV, picks, slots, held, staged, pairs, blocks, total, half, lambda p: None
    )
    put(AUX_DEV - 1, True, slots, total, staged)
    done = staged[pl.ds(place[2] * SIDE_SLOTS, SIDE_SLOTS)]
    out[...] = done.reshape(SIDE_SLOTS * ROWS, LANES).astype(jnp.bfloat16)


def join_kernel(place, staged, came, out):
    kept = staged[pl.ds((1 - place[2]) * SIDE_SLOTS, SIDE_SLOTS)].reshape(SIDE_SLOTS * ROWS, LANES)
    out[...] = (kept + came[...].astype(jnp.float32)).astype(jnp.bfloat16)


def join(place, staged, came):
    return pl.pallas_call(
        join_kernel,
        out_shape=jax.ShapeDtypeStruct(came.shape, came.dtype),
        in_specs=[SMEM] + [VMEM] * 2,
        out_specs=VMEM,
        compiler_params=pltpu.CompilerParams(vmem_limit_bytes=4 * MIB),
        cost_estimate=cost(0, 2 * MIB),
        name="join",
    )(place, staged, in_vmem(came))


STATE = [
    pltpu.VMEM(STAGED, jnp.float32),
    pltpu.VMEM(PAIRS, jnp.bfloat16),
    pltpu.VMEM((AUX_DEV, MS, PA, BS, OCC), jnp.bfloat16),
    pltpu.VMEM((BLOCKS, BS, OCC), jnp.bfloat16),
    pltpu.VMEM((2, MS * BS, MS * BS), jnp.float32),
]
HALF = pltpu.VMEM((2, MS * BS, CHUNK * OCC), jnp.bfloat16)
FLOPS = 2 * (MS * PA * BS * OCC * OCC * 4 + 2 * PA * OCC * (MS * BS) ** 2)


def early_products(count, picks, slots, rows, tensor, staged, pairs, held):
    return pl.pallas_call(
        early_kernel,
        out_shape=STATE,
        in_specs=[SMEM] * 3 + [VMEM] * 4 + [HBM] + [VMEM] * 3,
        out_specs=[VMEM] * 5,
        input_output_aliases={8: 0, 9: 1, 10: 2},
        scratch_shapes=[HALF, pltpu.SemaphoreType.DMA((AUX_DEV,))],
        compiler_params=pltpu.CompilerParams(vmem_limit_bytes=8 * MIB),
        cost_estimate=cost(FLOPS, 8 * MIB),
        name="early_products",
    )(count, picks, slots, *[in_vmem(r) for r in rows], in_hbm(tensor), staged, pairs, held)


def late_products(place, count, picks, slots, late, state):
    return pl.pallas_call(
        late_kernel,
        out_shape=STATE + [jax.ShapeDtypeStruct((SIDE_SLOTS * ROWS, LANES), jnp.bfloat16)],
        in_specs=[SMEM] * 4 + [VMEM] * 8,
        out_specs=[VMEM] * 6,
        input_output_aliases={7: 0, 8: 1, 9: 2, 10: 3, 11: 4},
        scratch_shapes=[HALF],
        compiler_params=pltpu.CompilerParams(vmem_limit_bytes=8 * MIB),
        cost_estimate=cost(FLOPS, 8 * MIB),
        name="late_products",
    )(place, count, picks, slots, *[in_vmem(r) for r in late], *state)


def locate_kernel(place, tables0, tables1, tables2, tables3, where):
    none = 1 << 20
    lane = lax.broadcasted_iota(jnp.int32, (AUX, LANES), 1)
    left = []
    for p in range(AUX_DEV):
        row = jnp.concatenate(
            [tables[:, p, :] for tables in (tables0, tables1, tables2, tables3)], axis=0
        )
        mark = (p * LANES + lane) * OWN_DEV + (row & (OWN_DEV - 1))
        left.append(jnp.where((row >> 4) == place[3], mark, none))
    found = jnp.zeros((AUX, LANES), jnp.int32)
    for k in range(CAP):
        least = jnp.minimum(jnp.minimum(left[0], left[1]), jnp.minimum(left[2], left[3]))
        least = jnp.min(least, axis=1, keepdims=True)
        found = jnp.where(lane == k, least & (OWN_DEV - 1), found)
        left = [jnp.where(v > least, v, none) for v in left]
    where[...] = found


def locate(place, every):
    return pl.pallas_call(
        locate_kernel,
        out_shape=jax.ShapeDtypeStruct((AUX, LANES), jnp.int32),
        in_specs=[SMEM] + [VMEM] * 4,
        out_specs=VMEM,
        compiler_params=pltpu.CompilerParams(vmem_limit_bytes=2 * MIB),
        cost_estimate=cost(0, 64 * 1024),
        name="locate",
    )(place, *every)


def collect_kernel(place, where, incoming, out, total):
    total[...] = jnp.zeros_like(total)
    for a in range(AUX):
        x, y = a % SIDE, a // SIDE
        even = place[2] == 1
        i = (place[0] - jnp.where(even, x, y)) & 3
        j = (place[1] - jnp.where(even, y, x)) & 3
        rows = incoming[pl.ds(a * SIDE * CAP * ROWS, SIDE * CAP * ROWS), :].astype(jnp.float32)
        summed = jnp.sum(rows.reshape(SIDE, CAP * ROWS, LANES), axis=0)
        for k in range(CAP):
            total[where[i * SIDE + j, k]] += summed[k * ROWS : (k + 1) * ROWS, :]
    for r in range(ROWS):
        line = total[:, r, :]
        for j in range(BS // ROWS):
            out[:, pl.ds((j * ROWS + r) * BS, BS)] = line[:, j * BS : (j + 1) * BS]


def collect(place, where, incoming):
    return pl.pallas_call(
        collect_kernel,
        out_shape=jax.ShapeDtypeStruct((OWN_DEV, BS * BS), jnp.float32),
        in_specs=[SMEM, SMEM, VMEM],
        out_specs=VMEM,
        scratch_shapes=[pltpu.VMEM((OWN_DEV, ROWS, LANES), jnp.float32)],
        compiler_params=pltpu.CompilerParams(vmem_limit_bytes=16 * MIB),
        name="collect",
    )(place, where, incoming)


def body(three_center, orbitals, partners, pair_owner):
    aux, orb = lax.axis_index("aux"), lax.axis_index("orb")
    x, y = aux % SIDE, aux // SIDE
    even = orb % 2 == 0
    near, far = jnp.where(even, x, y), jnp.where(even, y, x)
    own = orbitals.reshape(BLK_DEV, BS, OCC)

    got = [lax.ppermute(own, AXES, shifted(-j, True)) for j in (1, 2, 3)]

    place = jnp.stack([near, far, even.astype(jnp.int32), aux * ORB + orb]).astype(jnp.int32)
    mine, *sent, picks, slots, count = plan(place, partners, pair_owner)
    received = [lax.ppermute(sent[j - 1], AXES, shifted(j, False)) for j in (1, 2, 3)]

    here = stage(own, count)
    *early, shards = pack_early(received, here, got)
    early = [lax.ppermute(early[j - 1], AXES, shifted(-j, False)) for j in (1, 2, 3)]
    row0, *late, tables = pack_late(mine, received, shards)
    held, staged, pairs = head(three_center, row0)
    late = [lax.ppermute(late[j - 1], AXES, shifted(-j, False)) for j in (1, 2, 3)]
    every = [tables] + [lax.ppermute(tables, AXES, shifted(j, True)) for j in (1, 2, 3)]

    state = early_products(
        count, picks, slots, (row0, *early), three_center, staged, pairs, held
    )
    state = late_products(place, count, picks, slots, late, state)
    swap = [(device, device ^ 1) for device in range(DEVS)]
    outgoing = join(place, state[0], lax.ppermute(state[5], AXES, swap))
    cores = [list(range(core, DEVS, 2)) for core in range(2)]
    incoming = lax.all_to_all(
        outgoing, AXES, split_axis=0, concat_axis=0, axis_index_groups=cores, tiled=True
    )

    return collect(place, locate(place, every), incoming)


def solution(mesh):
    in_specs = (
        P("aux", None, None, None, None),
        P("aux", "orb"),
        P("aux", None, None),
        P("aux", None),
    )
    out_specs = P(("aux", "orb"), None)
    return jax.shard_map(body, mesh=mesh, in_specs=in_specs, out_specs=out_specs, check_vma=False)
```

```python
import functools

import jax
import jax.numpy as jnp
import numpy as np
from jax import lax
from jax.experimental import pallas as pl
from jax.experimental.pallas import tpu as pltpu
from jax.sharding import PartitionSpec as P

BS = 32
PA = 64
MS = 8
NPS = 4
AUX_DEV = 4
NOCC = 1024
BLK_DEV = 64
OWN_DEV = 16
CAP = 3
FETCH = 16
EP = MS * (MS - 1)
E = AUX_DEV * EP
ENTRIES = AUX_DEV * MS * NPS
OCC = 128
SIDE = 4
AUX = SIDE * SIDE
ORB = 8
DEVS = AUX * ORB
ROW_CAP = SIDE * FETCH
EARLY = 32
LATE = ROW_CAP - EARLY
ROWS = 8
CHUNK = 8
LANES = 128
AXES = ("aux", "orb")


def shifted(step, near):
    pairs = []
    for aux in range(AUX):
        x, y = aux % SIDE, aux // SIDE
        for orb in range(ORB):
            if (orb % 2 == 0) == near:
                to = y * SIDE + (x + step) % SIDE
            else:
                to = ((y + step) % SIDE) * SIDE + x
            pairs.append((aux * ORB + orb, to * ORB + orb))
    return pairs


def in_vmem(array):
    return pltpu.with_memory_space_constraint(array, pltpu.VMEM)


def in_hbm(array):
    return pltpu.with_memory_space_constraint(array, pltpu.HBM)


VMEM = pl.BlockSpec(memory_space=pltpu.VMEM)
SMEM = pl.BlockSpec(memory_space=pltpu.SMEM)
HBM = pl.BlockSpec(memory_space=pltpu.HBM)
MIB = 1024 * 1024
LIST_ROW = AUX_DEV
SIDE_SLOTS = DEVS * CAP // 2
BLOCKS = ROW_CAP + 3 * ROW_CAP
SOON = ROW_CAP + 3 * EARLY


def cost(flops, moved):
    return pl.CostEstimate(flops=flops, bytes_accessed=moved, transcendentals=0)


def columns(row):
    return jnp.broadcast_to(row, (LANES, LANES)).T


def plan_kernel(place, partners, owners, sent0, sent1, sent2, sent3, picks, slots, count):
    near, far, even = place[0], place[1], place[2]
    table = jnp.full((ROWS, LANES), -1, jnp.int32)
    for sent in (sent0, sent1, sent2, sent3):
        sent[...] = table
        sent[pl.ds(0, AUX_DEV), pl.ds(0, EP)] = owners[...]

    named = partners[...].reshape(AUX_DEV * MS, NPS)
    at = lax.broadcasted_iota(jnp.int32, (AUX_DEV * MS, LANES), 0) * NPS
    lane = lax.broadcasted_iota(jnp.int32, (AUX_DEV * MS, LANES), 1)
    spread = jnp.zeros((AUX_DEV * MS, LANES), jnp.int32)
    for k in range(NPS):
        spread += jnp.where(lane == at + k, named[:, k : k + 1], 0)
    wanted = jnp.sum(spread, axis=0, keepdims=True)

    down = lax.broadcasted_iota(jnp.int32, (LANES, LANES), 0)
    across = lax.broadcasted_iota(jnp.int32, (LANES, LANES), 1)
    earlier = down < across
    source, local = wanted >> 6, wanted & 63
    source_x, source_y = source & 3, source >> 2
    rel_near = (source_y + even * (source_x - source_y) - near) & 3
    rel_far = (source_x + even * (source_y - source_x) - far) & 3
    same = (columns(rel_far) == rel_far) & earlier
    rank = jnp.sum(same.astype(jnp.int32), axis=0, keepdims=True)
    packed = columns((rel_far * ROW_CAP + rank) * 256 + rel_near * BLK_DEV + local)
    key, value = packed >> 8, packed & 255
    for both, sends in enumerate(((sent0, sent1), (sent2, sent3))):
        line = jnp.sum(jnp.where(key == across + both * LANES, value, 0), axis=0, keepdims=True)
        for sent in sends:
            sent[pl.ds(LIST_ROW, 1), :] = line

    there = rel_far - 1
    remote = jnp.where(
        rank < EARLY, ROW_CAP + there * EARLY + rank, SOON + there * LATE + rank - EARLY
    )
    pick = jnp.where(rel_far == 0, rank, remote)
    picks[...] = pick
    missing = jnp.where(pick >= SOON, across[:1], LANES)
    count[...] = jnp.broadcast_to(jnp.min(missing, axis=1, keepdims=True) >> 5, (1, LANES))

    owner = sent0[...] >> 4
    stood = []
    for p in range(AUX_DEV):
        row = owner[p : p + 1]
        column = columns(row)
        hits = ((column == row) & earlier).astype(jnp.int32)
        for before in stood:
            hits += (before == row).astype(jnp.int32)
        at = (row & 1) * SIDE_SLOTS + (row >> 1) * CAP
        slots[pl.ds(p, 1), :] = at + jnp.sum(hits, axis=0, keepdims=True)
        stood.append(column)


def plan(place, partners, owners):
    tile = jax.ShapeDtypeStruct((ROWS, LANES), jnp.int32)
    line = jax.ShapeDtypeStruct((1, LANES), jnp.int32)
    return pl.pallas_call(
        plan_kernel,
        out_shape=[tile] * 4 + [line, tile, line],
        in_specs=[SMEM] + [VMEM] * 2,
        out_specs=[VMEM] * 7,
        compiler_params=pltpu.CompilerParams(vmem_limit_bytes=2 * MIB),
        cost_estimate=cost(0, 64 * 1024),
        name="plan",
    )(place, partners, owners)


STAGED = (DEVS * CAP + 1, ROWS, LANES)
PAIRS = (2, MS // 2, 2 * OCC, 2 * OCC)


def stage_kernel(tensor, own, picks, slots, count, held, own_out, staged, pairs, sems):
    del picks, slots, count
    copies = [
        pltpu.make_async_copy(own, own_out, sems.at[0]),
        pltpu.make_async_copy(tensor.at[0], held.at[0], sems.at[1]),
    ]
    for copy in copies:
        copy.start()
    staged[...] = jnp.zeros_like(staged)
    pairs[...] = jnp.zeros_like(pairs)
    for copy in copies:
        copy.wait()


def stage(tensor, own, *lists):
    return pl.pallas_call(
        stage_kernel,
        out_shape=[
            pltpu.VMEM(tensor.shape, tensor.dtype),
            pltpu.VMEM(own.shape, own.dtype),
            pltpu.VMEM(STAGED, jnp.float32),
            pltpu.VMEM(PAIRS, jnp.bfloat16),
        ],
        in_specs=[HBM] * 2 + [SMEM] * 3,
        out_specs=[VMEM] * 4,
        scratch_shapes=[pltpu.SemaphoreType.DMA((2,))],
        compiler_params=pltpu.CompilerParams(vmem_limit_bytes=MIB),
        cost_estimate=cost(0, 5 * MIB),
        name="stage",
    )(in_hbm(tensor), in_hbm(own), *lists)


def pack_early_kernel(
    req1, req2, req3, own, got1, got2, got3, out1, out2, out3, shards
):
    for at, src in enumerate((own, got1, got2, got3)):
        shards[pl.ds(at * BLK_DEV, BLK_DEV)] = src[...]
    for j, (req, out) in enumerate(((req1, out1), (req2, out2), (req3, out3))):

        @pl.loop(0, EARLY, unroll=8)
        def _(r):
            out[r] = shards[req[LIST_ROW, (j + 1) % 2 * ROW_CAP + r]]


def block_array(rows):
    return pltpu.VMEM((rows, BS, OCC), jnp.bfloat16)


def pack_early(received, own, got):
    return pl.pallas_call(
        pack_early_kernel,
        out_shape=[block_array(EARLY)] * 3 + [block_array(SIDE * BLK_DEV)],
        in_specs=[SMEM] * 3 + [VMEM] * 4,
        out_specs=[VMEM] * 4,
        compiler_params=pltpu.CompilerParams(vmem_limit_bytes=2 * MIB),
        cost_estimate=cost(0, 4 * MIB),
        name="pack_early",
    )(*received, own, *[in_vmem(g) for g in got])


def pack_late_kernel(
    req0, req1, req2, req3, shards, mine, tab1, tab2, tab3, out0, out1, out2, out3, tables
):
    for at, src in enumerate((mine, tab1, tab2, tab3)):
        tables[at] = src[...]
    for j, (req, out) in enumerate(((req1, out1), (req2, out2), (req3, out3))):

        @pl.loop(0, LATE, unroll=8)
        def _(r):
            out[r] = shards[req[LIST_ROW, (j + 1) % 2 * ROW_CAP + EARLY + r]]

    @pl.loop(0, ROW_CAP, unroll=8)
    def _(r):
        out0[r] = shards[req0[LIST_ROW, r]]


def pack_late(mine, received, shards):
    return pl.pallas_call(
        pack_late_kernel,
        out_shape=[block_array(ROW_CAP)]
        + [block_array(LATE)] * 3
        + [
            pltpu.VMEM((SIDE, ROWS, LANES), jnp.int32),
        ],
        in_specs=[SMEM] * 4 + [VMEM] * 5,
        out_specs=[VMEM] * 5,
        compiler_params=pltpu.CompilerParams(vmem_limit_bytes=2 * MIB),
        cost_estimate=cost(0, 2 * MIB),
        name="pack_late",
    )(mine, *received, shards, mine, *received)


def run_blocks(low, high, picks, slots, tensor, staged, pairs, blocks, total, half, ready):
    def fill(p):
        for s in range(MS):
            side = (s % 2) * OCC
            for k in range(NPS):
                pairs[p % 2, s // 2, pl.ds(side + k * BS, BS), pl.ds(side, OCC)] = blocks[
                    picks[0, (p * MS + s) * NPS + k]
                ]

    def first(p, c):
        for pair in range(MS // 2):
            left = jnp.concatenate(
                [
                    tensor[p, 2 * pair + side, pl.ds(c * CHUNK, CHUNK)].reshape(CHUNK * BS, OCC)
                    for side in range(2)
                ],
                axis=1,
            )
            both = jnp.dot(left, pairs[p % 2, pair], preferred_element_type=jnp.float32)
            both = both.astype(jnp.bfloat16)
            for side in range(2):
                for a in range(CHUNK):
                    half[c % 2, pl.ds((2 * pair + side) * BS, BS), pl.ds(a * OCC, OCC)] = both[
                        a * BS : (a + 1) * BS, side * OCC : (side + 1) * OCC
                    ]

    def second(p, c):
        slab = half[c % 2]
        product = lax.dot_general(
            slab, slab, (((1,), (1,)), ((), ())), preferred_element_type=jnp.float32
        )
        if c == 0:
            total[p % 2] = product
        else:
            total[p % 2] += product

    @pl.when(low < high)
    def _():
        fill(low)

    last = PA // CHUNK

    @pl.loop(low, high)
    def _(p):
        ready(p)
        first(p, 0)
        for c in range(last):
            if c + 1 < last:
                first(p, c + 1)
            second(p, c)
            if c == 0:
                put(jnp.maximum(p - 1, 0), p > 0, slots, total, staged)
            if c == 1:
                fill(jnp.minimum(p + 1, high - 1))


def put(p, valid, slots, total, staged):
    factor = np.float32(1.0 / np.sqrt(PA * NOCC))
    e = 0
    for s in range(MS):
        for t in range(MS):
            if s == t:
                continue
            tile = jnp.concatenate(
                [
                    total[p % 2, pl.ds(s * BS + j * ROWS, ROWS), pl.ds(t * BS, BS)]
                    for j in range(BS // ROWS)
                ],
                axis=1,
            )
            staged[jnp.where(valid, slots[p, e], DEVS * CAP)] = tile * factor
            e += 1


def early_kernel(
    count, picks, slots, row0, row1, row2, row3, tensor, staged0, pairs0, held0,
    staged, pairs, held, blocks, total, half, sems,
):
    del staged0, pairs0, held0

    def rest(p):
        return pltpu.make_async_copy(tensor.at[p], held.at[p], sems.at[p])

    for p in range(1, AUX_DEV):
        rest(p).start()
    blocks[pl.ds(0, ROW_CAP)] = row0[...]
    for at, src in enumerate((row1, row2, row3)):
        blocks[pl.ds(ROW_CAP + at * EARLY, EARLY)] = src[...]

    def ready(p):
        @pl.when(p > 0)
        def _():
            rest(p).wait()

    run_blocks(0, count[0, 0], picks, slots, held, staged, pairs, blocks, total, half, ready)
    for p in range(1, AUX_DEV):

        @pl.when(p >= count[0, 0])
        def _():
            rest(p).wait()


def late_kernel(
    place, count, picks, slots, late1, late2, late3, staged0, pairs0, held0, blocks0, total0,
    staged, pairs, held, blocks, total, out, half,
):
    del staged0, pairs0, held0, blocks0, total0
    for at, src in enumerate((late1, late2, late3)):
        blocks[pl.ds(SOON + at * LATE, LATE)] = src[...]
    run_blocks(
        count[0, 0], AUX_DEV, picks, slots, held, staged, pairs, blocks, total, half, lambda p: None
    )
    put(AUX_DEV - 1, True, slots, total, staged)
    done = staged[pl.ds(place[2] * SIDE_SLOTS, SIDE_SLOTS)]
    out[...] = done.reshape(SIDE_SLOTS * ROWS, LANES).astype(jnp.bfloat16)


def join_kernel(place, staged, came, out):
    kept = staged[pl.ds((1 - place[2]) * SIDE_SLOTS, SIDE_SLOTS)].reshape(SIDE_SLOTS * ROWS, LANES)
    out[...] = (kept + came[...].astype(jnp.float32)).astype(jnp.bfloat16)


def join(place, staged, came):
    return pl.pallas_call(
        join_kernel,
        out_shape=jax.ShapeDtypeStruct(came.shape, came.dtype),
        in_specs=[SMEM] + [VMEM] * 2,
        out_specs=VMEM,
        compiler_params=pltpu.CompilerParams(vmem_limit_bytes=4 * MIB),
        cost_estimate=cost(0, 2 * MIB),
        name="join",
    )(place, staged, in_vmem(came))


STATE = [
    pltpu.VMEM(STAGED, jnp.float32),
    pltpu.VMEM(PAIRS, jnp.bfloat16),
    pltpu.VMEM((AUX_DEV, MS, PA, BS, OCC), jnp.bfloat16),
    pltpu.VMEM((BLOCKS, BS, OCC), jnp.bfloat16),
    pltpu.VMEM((2, MS * BS, MS * BS), jnp.float32),
]
HALF = pltpu.VMEM((2, MS * BS, CHUNK * OCC), jnp.bfloat16)
FLOPS = 2 * (MS * PA * BS * OCC * OCC * 4 + 2 * PA * OCC * (MS * BS) ** 2)


def early_products(count, picks, slots, rows, tensor, staged, pairs, held):
    return pl.pallas_call(
        early_kernel,
        out_shape=STATE,
        in_specs=[SMEM] * 3 + [VMEM] * 4 + [HBM] + [VMEM] * 3,
        out_specs=[VMEM] * 5,
        input_output_aliases={8: 0, 9: 1, 10: 2},
        scratch_shapes=[HALF, pltpu.SemaphoreType.DMA((AUX_DEV,))],
        compiler_params=pltpu.CompilerParams(vmem_limit_bytes=8 * MIB),
        cost_estimate=cost(FLOPS, 8 * MIB),
        name="early_products",
    )(count, picks, slots, *[in_vmem(r) for r in rows], in_hbm(tensor), staged, pairs, held)


def late_products(place, count, picks, slots, late, state):
    return pl.pallas_call(
        late_kernel,
        out_shape=STATE + [jax.ShapeDtypeStruct((SIDE_SLOTS * ROWS, LANES), jnp.bfloat16)],
        in_specs=[SMEM] * 4 + [VMEM] * 8,
        out_specs=[VMEM] * 6,
        input_output_aliases={7: 0, 8: 1, 9: 2, 10: 3, 11: 4},
        scratch_shapes=[HALF],
        compiler_params=pltpu.CompilerParams(vmem_limit_bytes=8 * MIB),
        cost_estimate=cost(FLOPS, 8 * MIB),
        name="late_products",
    )(place, count, picks, slots, *[in_vmem(r) for r in late], *state)


def locate_kernel(place, tables0, tables1, tables2, tables3, where):
    none = 1 << 20
    lane = lax.broadcasted_iota(jnp.int32, (AUX, LANES), 1)
    left = []
    for p in range(AUX_DEV):
        row = jnp.concatenate(
            [tables[:, p, :] for tables in (tables0, tables1, tables2, tables3)], axis=0
        )
        mark = (p * LANES + lane) * OWN_DEV + (row & (OWN_DEV - 1))
        left.append(jnp.where((row >> 4) == place[3], mark, none))
    found = jnp.zeros((AUX, LANES), jnp.int32)
    for k in range(CAP):
        least = jnp.minimum(jnp.minimum(left[0], left[1]), jnp.minimum(left[2], left[3]))
        least = jnp.min(least, axis=1, keepdims=True)
        found = jnp.where(lane == k, least & (OWN_DEV - 1), found)
        left = [jnp.where(v > least, v, none) for v in left]
    where[...] = found


def locate(place, every):
    return pl.pallas_call(
        locate_kernel,
        out_shape=jax.ShapeDtypeStruct((AUX, LANES), jnp.int32),
        in_specs=[SMEM] + [VMEM] * 4,
        out_specs=VMEM,
        compiler_params=pltpu.CompilerParams(vmem_limit_bytes=2 * MIB),
        cost_estimate=cost(0, 64 * 1024),
        name="locate",
    )(place, *every)


def collect_kernel(place, where, incoming, out, total):
    total[...] = jnp.zeros_like(total)
    for a in range(AUX):
        x, y = a % SIDE, a // SIDE
        even = place[2] == 1
        i = (place[0] - jnp.where(even, x, y)) & 3
        j = (place[1] - jnp.where(even, y, x)) & 3
        rows = incoming[pl.ds(a * SIDE * CAP * ROWS, SIDE * CAP * ROWS), :].astype(jnp.float32)
        summed = jnp.sum(rows.reshape(SIDE, CAP * ROWS, LANES), axis=0)
        for k in range(CAP):
            total[where[i * SIDE + j, k]] += summed[k * ROWS : (k + 1) * ROWS, :]
    for r in range(ROWS):
        line = total[:, r, :]
        for j in range(BS // ROWS):
            out[:, pl.ds((j * ROWS + r) * BS, BS)] = line[:, j * BS : (j + 1) * BS]


def collect(place, where, incoming):
    return pl.pallas_call(
        collect_kernel,
        out_shape=jax.ShapeDtypeStruct((OWN_DEV, BS * BS), jnp.float32),
        in_specs=[SMEM, SMEM, VMEM],
        out_specs=VMEM,
        scratch_shapes=[pltpu.VMEM((OWN_DEV, ROWS, LANES), jnp.float32)],
        compiler_params=pltpu.CompilerParams(vmem_limit_bytes=16 * MIB),
        name="collect",
    )(place, where, incoming)


def body(three_center, orbitals, partners, pair_owner):
    aux, orb = lax.axis_index("aux"), lax.axis_index("orb")
    x, y = aux % SIDE, aux // SIDE
    even = orb % 2 == 0
    near, far = jnp.where(even, x, y), jnp.where(even, y, x)
    own = orbitals.reshape(BLK_DEV, BS, OCC)

    got = [lax.ppermute(own, AXES, shifted(-j, True)) for j in (1, 2, 3)]

    place = jnp.stack([near, far, even.astype(jnp.int32), aux * ORB + orb]).astype(jnp.int32)
    mine, *sent, picks, slots, count = plan(place, partners, pair_owner)
    received = [lax.ppermute(sent[j - 1], AXES, shifted(j, False)) for j in (1, 2, 3)]

    held, here, staged, pairs = stage(three_center, own, picks, slots, count)
    *early, shards = pack_early(received, here, got)
    early = [lax.ppermute(early[j - 1], AXES, shifted(-j, False)) for j in (1, 2, 3)]
    row0, *late, tables = pack_late(mine, received, shards)
    late = [lax.ppermute(late[j - 1], AXES, shifted(-j, False)) for j in (1, 2, 3)]
    every = [tables] + [lax.ppermute(tables, AXES, shifted(j, True)) for j in (1, 2, 3)]

    state = early_products(
        count, picks, slots, (row0, *early), three_center, staged, pairs, held
    )
    every, state = lax.optimization_barrier((every, state))
    state = late_products(place, count, picks, slots, late, state)
    swap = [(device, device ^ 1) for device in range(DEVS)]
    outgoing = join(place, state[0], lax.ppermute(state[5], AXES, swap))
    cores = [list(range(core, DEVS, 2)) for core in range(2)]
    incoming = lax.all_to_all(
        outgoing, AXES, split_axis=0, concat_axis=0, axis_index_groups=cores, tiled=True
    )

    return collect(place, locate(place, every), incoming)


def solution(mesh):
    in_specs = (
        P("aux", None, None, None, None),
        P("aux", "orb"),
        P("aux", None, None),
        P("aux", None),
    )
    out_specs = P(("aux", "orb"), None)
    return jax.shard_map(body, mesh=mesh, in_specs=in_specs, out_specs=out_specs, check_vma=False)
```

```python
import functools

import jax
import jax.numpy as jnp
import numpy as np
from jax import lax
from jax.experimental import pallas as pl
from jax.experimental.pallas import tpu as pltpu
from jax.sharding import PartitionSpec as P

BS = 32
PA = 64
MS = 8
NPS = 4
AUX_DEV = 4
NOCC = 1024
BLK_DEV = 64
OWN_DEV = 16
CAP = 3
FETCH = 16
EP = MS * (MS - 1)
E = AUX_DEV * EP
ENTRIES = AUX_DEV * MS * NPS
OCC = 128
SIDE = 4
AUX = SIDE * SIDE
ORB = 8
DEVS = AUX * ORB
ROW_CAP = SIDE * FETCH
EARLY = 32
LATE = ROW_CAP - EARLY
ROWS = 8
CHUNK = 8
LANES = 128
AXES = ("aux", "orb")


def shifted(step, near):
    pairs = []
    for aux in range(AUX):
        x, y = aux % SIDE, aux // SIDE
        for orb in range(ORB):
            if (orb % 2 == 0) == near:
                to = y * SIDE + (x + step) % SIDE
            else:
                to = ((y + step) % SIDE) * SIDE + x
            pairs.append((aux * ORB + orb, to * ORB + orb))
    return pairs


def in_vmem(array):
    return pltpu.with_memory_space_constraint(array, pltpu.VMEM)


def in_hbm(array):
    return pltpu.with_memory_space_constraint(array, pltpu.HBM)


VMEM = pl.BlockSpec(memory_space=pltpu.VMEM)
SMEM = pl.BlockSpec(memory_space=pltpu.SMEM)
HBM = pl.BlockSpec(memory_space=pltpu.HBM)
MIB = 1024 * 1024
LIST_ROW = AUX_DEV
SIDE_SLOTS = DEVS * CAP // 2
BLOCKS = ROW_CAP + 3 * ROW_CAP
SOON = ROW_CAP + 3 * EARLY


def cost(flops, moved):
    return pl.CostEstimate(flops=flops, bytes_accessed=moved, transcendentals=0)


def columns(row):
    return jnp.broadcast_to(row, (LANES, LANES)).T


def plan_kernel(place, partners, owners, sent0, sent1, sent2, sent3, picks, slots, count):
    near, far, even = place[0], place[1], place[2]
    table = jnp.full((ROWS, LANES), -1, jnp.int32)
    for sent in (sent0, sent1, sent2, sent3):
        sent[...] = table
        sent[pl.ds(0, AUX_DEV), pl.ds(0, EP)] = owners[...]

    named = partners[...].reshape(AUX_DEV * MS, NPS)
    at = lax.broadcasted_iota(jnp.int32, (AUX_DEV * MS, LANES), 0) * NPS
    lane = lax.broadcasted_iota(jnp.int32, (AUX_DEV * MS, LANES), 1)
    spread = jnp.zeros((AUX_DEV * MS, LANES), jnp.int32)
    for k in range(NPS):
        spread += jnp.where(lane == at + k, named[:, k : k + 1], 0)
    wanted = jnp.sum(spread, axis=0, keepdims=True)

    down = lax.broadcasted_iota(jnp.int32, (LANES, LANES), 0)
    across = lax.broadcasted_iota(jnp.int32, (LANES, LANES), 1)
    earlier = down < across
    source, local = wanted >> 6, wanted & 63
    source_x, source_y = source & 3, source >> 2
    rel_near = (source_y + even * (source_x - source_y) - near) & 3
    rel_far = (source_x + even * (source_y - source_x) - far) & 3
    same = (columns(rel_far) == rel_far) & earlier
    rank = jnp.sum(same.astype(jnp.int32), axis=0, keepdims=True)
    packed = columns((rel_far * ROW_CAP + rank) * 256 + rel_near * BLK_DEV + local)
    key, value = packed >> 8, packed & 255
    for both, sends in enumerate(((sent0, sent1), (sent2, sent3))):
        line = jnp.sum(jnp.where(key == across + both * LANES, value, 0), axis=0, keepdims=True)
        for sent in sends:
            sent[pl.ds(LIST_ROW, 1), :] = line

    there = rel_far - 1
    remote = jnp.where(
        rank < EARLY, ROW_CAP + there * EARLY + rank, SOON + there * LATE + rank - EARLY
    )
    pick = jnp.where(rel_far == 0, rank, remote)
    picks[...] = pick
    missing = jnp.where(pick >= SOON, across[:1], LANES)
    count[...] = jnp.broadcast_to(jnp.min(missing, axis=1, keepdims=True) >> 5, (1, LANES))

    owner = sent0[...] >> 4
    stood = []
    for p in range(AUX_DEV):
        row = owner[p : p + 1]
        column = columns(row)
        hits = ((column == row) & earlier).astype(jnp.int32)
        for before in stood:
            hits += (before == row).astype(jnp.int32)
        at = (row & 1) * SIDE_SLOTS + (row >> 1) * CAP
        slots[pl.ds(p, 1), :] = at + jnp.sum(hits, axis=0, keepdims=True)
        stood.append(column)


def plan(place, partners, owners):
    tile = jax.ShapeDtypeStruct((ROWS, LANES), jnp.int32)
    line = jax.ShapeDtypeStruct((1, LANES), jnp.int32)
    return pl.pallas_call(
        plan_kernel,
        out_shape=[tile] * 4 + [line, tile, line],
        in_specs=[SMEM] + [VMEM] * 2,
        out_specs=[VMEM] * 7,
        compiler_params=pltpu.CompilerParams(vmem_limit_bytes=2 * MIB),
        cost_estimate=cost(0, 64 * 1024),
        name="plan",
    )(place, partners, owners)


STAGED = (DEVS * CAP + 1, ROWS, LANES)
PAIRS = (2, MS // 2, 2 * OCC, 2 * OCC)


def stage_kernel(tensor, own, picks, slots, count, held, own_out, staged, pairs, sems):
    del picks, slots, count
    copies = [
        pltpu.make_async_copy(own, own_out, sems.at[0]),
        pltpu.make_async_copy(tensor.at[0], held.at[0], sems.at[1]),
    ]
    for copy in copies:
        copy.start()
    staged[...] = jnp.zeros_like(staged)
    pairs[...] = jnp.zeros_like(pairs)
    for copy in copies:
        copy.wait()


def stage(tensor, own, *lists):
    return pl.pallas_call(
        stage_kernel,
        out_shape=[
            pltpu.VMEM(tensor.shape, tensor.dtype),
            pltpu.VMEM(own.shape, own.dtype),
            pltpu.VMEM(STAGED, jnp.float32),
            pltpu.VMEM(PAIRS, jnp.bfloat16),
        ],
        in_specs=[HBM] * 2 + [SMEM] * 3,
        out_specs=[VMEM] * 4,
        scratch_shapes=[pltpu.SemaphoreType.DMA((2,))],
        compiler_params=pltpu.CompilerParams(vmem_limit_bytes=MIB),
        cost_estimate=cost(0, 5 * MIB),
        name="stage",
    )(in_hbm(tensor), in_hbm(own), *lists)


def pack_early_kernel(
    req1, req2, req3, own, got1, got2, got3, out1, out2, out3, shards
):
    for at, src in enumerate((own, got1, got2, got3)):
        shards[pl.ds(at * BLK_DEV, BLK_DEV)] = src[...]
    for j, (req, out) in enumerate(((req1, out1), (req2, out2), (req3, out3))):

        @pl.loop(0, EARLY, unroll=32)
        def _(r):
            out[r] = shards[req[LIST_ROW, (j + 1) % 2 * ROW_CAP + r]]


def block_array(rows):
    return pltpu.VMEM((rows, BS, OCC), jnp.bfloat16)


def pack_early(received, own, got):
    return pl.pallas_call(
        pack_early_kernel,
        out_shape=[block_array(EARLY)] * 3 + [block_array(SIDE * BLK_DEV)],
        in_specs=[SMEM] * 3 + [VMEM] * 4,
        out_specs=[VMEM] * 4,
        compiler_params=pltpu.CompilerParams(vmem_limit_bytes=2 * MIB),
        cost_estimate=cost(0, 4 * MIB),
        name="pack_early",
    )(*received, own, *[in_vmem(g) for g in got])


def pack_late_kernel(
    req0, req1, req2, req3, shards, mine, tab1, tab2, tab3, out0, out1, out2, out3, tables
):
    for at, src in enumerate((mine, tab1, tab2, tab3)):
        tables[at] = src[...]
    for j, (req, out) in enumerate(((req1, out1), (req2, out2), (req3, out3))):

        @pl.loop(0, LATE, unroll=32)
        def _(r):
            out[r] = shards[req[LIST_ROW, (j + 1) % 2 * ROW_CAP + EARLY + r]]

    @pl.loop(0, ROW_CAP, unroll=32)
    def _(r):
        out0[r] = shards[req0[LIST_ROW, r]]


def pack_late(mine, received, shards):
    return pl.pallas_call(
        pack_late_kernel,
        out_shape=[block_array(ROW_CAP)]
        + [block_array(LATE)] * 3
        + [
            pltpu.VMEM((SIDE, ROWS, LANES), jnp.int32),
        ],
        in_specs=[SMEM] * 4 + [VMEM] * 5,
        out_specs=[VMEM] * 5,
        compiler_params=pltpu.CompilerParams(vmem_limit_bytes=2 * MIB),
        cost_estimate=cost(0, 2 * MIB),
        name="pack_late",
    )(mine, *received, shards, mine, *received)


def run_blocks(low, high, picks, slots, tensor, staged, pairs, blocks, total, half, ready):
    def fill(p):
        for s in range(MS):
            side = (s % 2) * OCC
            for k in range(NPS):
                pairs[p % 2, s // 2, pl.ds(side + k * BS, BS), pl.ds(side, OCC)] = blocks[
                    picks[0, (p * MS + s) * NPS + k]
                ]

    def first(p, c):
        for pair in range(MS // 2):
            left = jnp.concatenate(
                [
                    tensor[p, 2 * pair + side, pl.ds(c * CHUNK, CHUNK)].reshape(CHUNK * BS, OCC)
                    for side in range(2)
                ],
                axis=1,
            )
            both = jnp.dot(left, pairs[p % 2, pair], preferred_element_type=jnp.float32)
            both = both.astype(jnp.bfloat16)
            for side in range(2):
                for a in range(CHUNK):
                    half[c % 2, pl.ds((2 * pair + side) * BS, BS), pl.ds(a * OCC, OCC)] = both[
                        a * BS : (a + 1) * BS, side * OCC : (side + 1) * OCC
                    ]

    def second(p, c):
        slab = half[c % 2]
        product = lax.dot_general(
            slab, slab, (((1,), (1,)), ((), ())), preferred_element_type=jnp.float32
        )
        if c == 0:
            total[p % 2] = product
        else:
            total[p % 2] += product

    @pl.when(low < high)
    def _():
        fill(low)

    last = PA // CHUNK

    @pl.loop(low, high)
    def _(p):
        ready(p)
        first(p, 0)
        for c in range(last):
            if c + 1 < last:
                first(p, c + 1)
            second(p, c)
            if c == 0:
                put(jnp.maximum(p - 1, 0), p > 0, slots, total, staged)
            if c == 1:
                fill(jnp.minimum(p + 1, high - 1))


def put(p, valid, slots, total, staged):
    factor = np.float32(1.0 / np.sqrt(PA * NOCC))
    e = 0
    for s in range(MS):
        for t in range(MS):
            if s == t:
                continue
            tile = jnp.concatenate(
                [
                    total[p % 2, pl.ds(s * BS + j * ROWS, ROWS), pl.ds(t * BS, BS)]
                    for j in range(BS // ROWS)
                ],
                axis=1,
            )
            staged[jnp.where(valid, slots[p, e], DEVS * CAP)] = tile * factor
            e += 1


def early_kernel(
    count, picks, slots, row0, row1, row2, row3, tensor, staged0, pairs0, held0,
    staged, pairs, held, blocks, total, half, sems,
):
    del staged0, pairs0, held0

    def rest(p):
        return pltpu.make_async_copy(tensor.at[p], held.at[p], sems.at[p])

    for p in range(1, AUX_DEV):
        rest(p).start()
    blocks[pl.ds(0, ROW_CAP)] = row0[...]
    for at, src in enumerate((row1, row2, row3)):
        blocks[pl.ds(ROW_CAP + at * EARLY, EARLY)] = src[...]

    def ready(p):
        @pl.when(p > 0)
        def _():
            rest(p).wait()

    run_blocks(0, count[0, 0], picks, slots, held, staged, pairs, blocks, total, half, ready)
    for p in range(1, AUX_DEV):

        @pl.when(p >= count[0, 0])
        def _():
            rest(p).wait()


def late_kernel(
    place, count, picks, slots, late1, late2, late3, staged0, pairs0, held0, blocks0, total0,
    staged, pairs, held, blocks, total, out, half,
):
    del staged0, pairs0, held0, blocks0, total0
    for at, src in enumerate((late1, late2, late3)):
        blocks[pl.ds(SOON + at * LATE, LATE)] = src[...]
    run_blocks(
        count[0, 0], AUX_DEV, picks, slots, held, staged, pairs, blocks, total, half, lambda p: None
    )
    put(AUX_DEV - 1, True, slots, total, staged)
    done = staged[pl.ds(place[2] * SIDE_SLOTS, SIDE_SLOTS)]
    out[...] = done.reshape(SIDE_SLOTS * ROWS, LANES).astype(jnp.bfloat16)


def join_kernel(place, staged, came, out):
    kept = staged[pl.ds((1 - place[2]) * SIDE_SLOTS, SIDE_SLOTS)].reshape(SIDE_SLOTS * ROWS, LANES)
    out[...] = (kept + came[...].astype(jnp.float32)).astype(jnp.bfloat16)


def join(place, staged, came):
    return pl.pallas_call(
        join_kernel,
        out_shape=jax.ShapeDtypeStruct(came.shape, came.dtype),
        in_specs=[SMEM] + [VMEM] * 2,
        out_specs=VMEM,
        compiler_params=pltpu.CompilerParams(vmem_limit_bytes=4 * MIB),
        cost_estimate=cost(0, 2 * MIB),
        name="join",
    )(place, staged, in_vmem(came))


STATE = [
    pltpu.VMEM(STAGED, jnp.float32),
    pltpu.VMEM(PAIRS, jnp.bfloat16),
    pltpu.VMEM((AUX_DEV, MS, PA, BS, OCC), jnp.bfloat16),
    pltpu.VMEM((BLOCKS, BS, OCC), jnp.bfloat16),
    pltpu.VMEM((2, MS * BS, MS * BS), jnp.float32),
]
HALF = pltpu.VMEM((2, MS * BS, CHUNK * OCC), jnp.bfloat16)
FLOPS = 2 * (MS * PA * BS * OCC * OCC * 4 + 2 * PA * OCC * (MS * BS) ** 2)


def early_products(count, picks, slots, rows, tensor, staged, pairs, held):
    return pl.pallas_call(
        early_kernel,
        out_shape=STATE,
        in_specs=[SMEM] * 3 + [VMEM] * 4 + [HBM] + [VMEM] * 3,
        out_specs=[VMEM] * 5,
        input_output_aliases={8: 0, 9: 1, 10: 2},
        scratch_shapes=[HALF, pltpu.SemaphoreType.DMA((AUX_DEV,))],
        compiler_params=pltpu.CompilerParams(vmem_limit_bytes=8 * MIB),
        cost_estimate=cost(FLOPS, 8 * MIB),
        name="early_products",
    )(count, picks, slots, *[in_vmem(r) for r in rows], in_hbm(tensor), staged, pairs, held)


def late_products(place, count, picks, slots, late, state):
    return pl.pallas_call(
        late_kernel,
        out_shape=STATE + [jax.ShapeDtypeStruct((SIDE_SLOTS * ROWS, LANES), jnp.bfloat16)],
        in_specs=[SMEM] * 4 + [VMEM] * 8,
        out_specs=[VMEM] * 6,
        input_output_aliases={7: 0, 8: 1, 9: 2, 10: 3, 11: 4},
        scratch_shapes=[HALF],
        compiler_params=pltpu.CompilerParams(vmem_limit_bytes=8 * MIB),
        cost_estimate=cost(FLOPS, 8 * MIB),
        name="late_products",
    )(place, count, picks, slots, *[in_vmem(r) for r in late], *state)


def locate_kernel(place, tables0, tables1, tables2, tables3, where):
    none = 1 << 20
    lane = lax.broadcasted_iota(jnp.int32, (AUX, LANES), 1)
    left = []
    for p in range(AUX_DEV):
        row = jnp.concatenate(
            [tables[:, p, :] for tables in (tables0, tables1, tables2, tables3)], axis=0
        )
        mark = (p * LANES + lane) * OWN_DEV + (row & (OWN_DEV - 1))
        left.append(jnp.where((row >> 4) == place[3], mark, none))
    found = jnp.zeros((AUX, LANES), jnp.int32)
    for k in range(CAP):
        least = jnp.minimum(jnp.minimum(left[0], left[1]), jnp.minimum(left[2], left[3]))
        least = jnp.min(least, axis=1, keepdims=True)
        found = jnp.where(lane == k, least & (OWN_DEV - 1), found)
        left = [jnp.where(v > least, v, none) for v in left]
    where[...] = found


def locate(place, every):
    return pl.pallas_call(
        locate_kernel,
        out_shape=jax.ShapeDtypeStruct((AUX, LANES), jnp.int32),
        in_specs=[SMEM] + [VMEM] * 4,
        out_specs=VMEM,
        compiler_params=pltpu.CompilerParams(vmem_limit_bytes=2 * MIB),
        cost_estimate=cost(0, 64 * 1024),
        name="locate",
    )(place, *every)


def collect_kernel(place, where, incoming, out, total):
    total[...] = jnp.zeros_like(total)
    for a in range(AUX):
        x, y = a % SIDE, a // SIDE
        even = place[2] == 1
        i = (place[0] - jnp.where(even, x, y)) & 3
        j = (place[1] - jnp.where(even, y, x)) & 3
        rows = incoming[pl.ds(a * SIDE * CAP * ROWS, SIDE * CAP * ROWS), :].astype(jnp.float32)
        summed = jnp.sum(rows.reshape(SIDE, CAP * ROWS, LANES), axis=0)
        for k in range(CAP):
            total[where[i * SIDE + j, k]] += summed[k * ROWS : (k + 1) * ROWS, :]
    for r in range(ROWS):
        line = total[:, r, :]
        for j in range(BS // ROWS):
            out[:, pl.ds((j * ROWS + r) * BS, BS)] = line[:, j * BS : (j + 1) * BS]


def collect(place, where, incoming):
    return pl.pallas_call(
        collect_kernel,
        out_shape=jax.ShapeDtypeStruct((OWN_DEV, BS * BS), jnp.float32),
        in_specs=[SMEM, SMEM, VMEM],
        out_specs=VMEM,
        scratch_shapes=[pltpu.VMEM((OWN_DEV, ROWS, LANES), jnp.float32)],
        compiler_params=pltpu.CompilerParams(vmem_limit_bytes=16 * MIB),
        name="collect",
    )(place, where, incoming)


def body(three_center, orbitals, partners, pair_owner):
    aux, orb = lax.axis_index("aux"), lax.axis_index("orb")
    x, y = aux % SIDE, aux // SIDE
    even = orb % 2 == 0
    near, far = jnp.where(even, x, y), jnp.where(even, y, x)
    own = orbitals.reshape(BLK_DEV, BS, OCC)

    got = [lax.ppermute(own, AXES, shifted(-j, True)) for j in (1, 2, 3)]

    place = jnp.stack([near, far, even.astype(jnp.int32), aux * ORB + orb]).astype(jnp.int32)
    mine, *sent, picks, slots, count = plan(place, partners, pair_owner)
    received = [lax.ppermute(sent[j - 1], AXES, shifted(j, False)) for j in (1, 2, 3)]

    held, here, staged, pairs = stage(three_center, own, picks, slots, count)
    *early, shards = pack_early(received, here, got)
    early = [lax.ppermute(early[j - 1], AXES, shifted(-j, False)) for j in (1, 2, 3)]
    row0, *late, tables = pack_late(mine, received, shards)
    late = [lax.ppermute(late[j - 1], AXES, shifted(-j, False)) for j in (1, 2, 3)]
    every = [tables] + [lax.ppermute(tables, AXES, shifted(j, True)) for j in (1, 2, 3)]

    state = early_products(
        count, picks, slots, (row0, *early), three_center, staged, pairs, held
    )
    state = late_products(place, count, picks, slots, late, state)
    swap = [(device, device ^ 1) for device in range(DEVS)]
    outgoing = join(place, state[0], lax.ppermute(state[5], AXES, swap))
    cores = [list(range(core, DEVS, 2)) for core in range(2)]
    incoming = lax.all_to_all(
        outgoing, AXES, split_axis=0, concat_axis=0, axis_index_groups=cores, tiled=True
    )

    return collect(place, locate(place, every), incoming)


def solution(mesh):
    in_specs = (
        P("aux", None, None, None, None),
        P("aux", "orb"),
        P("aux", None, None),
        P("aux", None),
    )
    out_specs = P(("aux", "orb"), None)
    return jax.shard_map(body, mesh=mesh, in_specs=in_specs, out_specs=out_specs, check_vma=False)
```
